32 devices in a mesh: seq: 8 (over z, x), tp: 4 (over y, core).
Axes of the slice: x: 2, y: 2, z: 4, core: 2. Of those that a mesh axis runs over, the one named last changes fastest.
Arguments:
- tokens: bfloat16 [2, 2048, 2048], P(None, 'seq', 'tp'), may hold values from -6 to 6
- norm_gain: bfloat16 [2, 2048], P(None, 'tp'), may hold values from 0.5 to 1.5
- input_weight: bfloat16 [2, 2048, 2, 4096], P(None, None, None, 'tp'), may hold values from -0.125 to 0.125
- conv_weight: bfloat16 [2, 4, 4096], P(None, None, 'tp'), may hold values from -3 to 3
- conv_bias: bfloat16 [2, 4096], P(None, 'tp'), may hold values from -3 to 3
- select_weight: bfloat16 [2, 4096, 160], P(None, 'tp'), may hold values from -0.09375 to 0.09375
- step_weight: bfloat16 [2, 128, 4096], P(None, None, 'tp'), may hold values from -0.5 to 0.5
- step_bias: float32 [2, 4096], P(None, 'tp'), may hold values from -9 to -2.3
- skip_gain: bfloat16 [2, 4096], P(None, 'tp'), may hold values from 0.5 to 1.5
- out_weight: bfloat16 [2, 4096, 2048], P(None, 'tp'), may hold values from -0.25 to 0.25
- cotangent: bfloat16 [2, 2048, 2048], P(None, 'seq', 'tp'), may hold values from -6 to 6
- doc_lengths: int32 [2, 64], replicated, may hold values from 0 to 2048, as said below
- doc_offsets: int32 [2, 64], replicated, may hold values from 0 to 2048, as said below
Outputs:
- layer_out: bfloat16 [2, 2048, 2048], P(None, 'seq', 'tp')
- tokens_grad: bfloat16 [2, 2048, 2048], P(None, 'seq', 'tp')
- gain_grad: float32 [2, 2048], P(None, 'tp')
- inweight_grad: float32 [2, 2048, 2, 4096], P(None, 'seq', None, 'tp')
- convweight_grad: float32 [2, 4, 4096], P(None, None, 'tp')
- convbias_grad: float32 [2, 4096], P(None, 'tp')
- select_grad: float32 [2, 4096, 128], P(None, 'tp', 'seq')
- keyquery_grad: float32 [2, 4096, 32], P(None, 'tp')
- step_grad: float32 [2, 128, 4096], P(None, 'seq', 'tp')
- stepbias_grad: float32 [2, 4096], P(None, 'tp')
- skip_grad: float32 [2, 4096], P(None, 'tp')
- outweight_grad: float32 [2, 4096, 2048], P(None, 'tp', 'seq')
The draws below stay inside these ranges and needn't reach their ends.
Inputs may be any that keep to these rules, and one draw needn't show every extreme that they name: `doc_offsets`: in each micro-batch the slots' offsets do not fall and start at 0; a document fills positions offset to offset + length - 1, before the next slot's offset, and positions between documents are padding. Slots that hold no document have offset 2048 and length 0. In one micro-batch, drawn from the seed, a single document fills all 2048 positions; in the others documents are 64 to 1024 positions long, except one cut by the stream's end. `doc_lengths`: lengths of the slots described with doc_offsets.
All inputs are finite; a program needn't handle non-finite values.
Results may differ from the reference program's by a relative error of at most 0.03.
Values may be sent and summed in bfloat16 or wider, within the bound.
No kernel may reach another device: no remote copies, remote signals or barrier semaphores. Data moves between devices by JAX's collectives and lax.ppermute only.
A program may use at most 320 MiB of HBM per device.

```python
import math
import jax
import jax.numpy as jnp
from jax import lax

D = 2048
INNER = 4096
STATE = 16
CONV = 4
RANK = 128
LAYERS = 2
MB = 2
MIN_DOC = 64
NDOC = 64
TOKENS = 2048
MAX_DOC = 1024


def packing(key):
    key = jax.random.fold_in(key, 5)
    pick_key, length_key, scale_key, spacing_key = jax.random.split(key, 4)
    spanning = jax.random.randint(pick_key, (), 0, MB)
    exponent = jax.random.randint(scale_key, (MB, NDOC), 0, 8)
    base_length = MIN_DOC * jnp.left_shift(jnp.ones((MB, NDOC), jnp.int32), exponent)
    extra_length = jax.random.randint(length_key, (MB, NDOC), 0, 1 << 30) % base_length
    drawn_length = jnp.minimum(base_length + extra_length, MAX_DOC)
    spacing = jax.random.randint(spacing_key, (MB, NDOC), 0, MIN_DOC // 2 + 1)
    stride = drawn_length + spacing
    raw_offsets = jnp.cumsum(stride, axis=1) - stride
    offsets = jnp.minimum(raw_offsets, TOKENS)
    lengths = jnp.minimum(drawn_length, TOKENS - offsets)
    column = jnp.arange(NDOC)[None, :]
    chosen = (jnp.arange(MB) == spanning)[:, None]
    offsets = jnp.where(chosen, jnp.where(column == 0, 0, TOKENS), offsets)
    lengths = jnp.where(chosen, jnp.where(column == 0, TOKENS, 0), lengths)
    return (lengths.astype(jnp.int32), offsets.astype(jnp.int32))


def draw_doc_lengths(key, part):
    return packing(key)[0]


def draw_doc_offsets(key, part):
    return packing(key)[1]


def steps_of(own_key, dims, cuts, smallest, largest):
    def one(axis_at, blocks):
        draws = jax.random.uniform(jax.random.fold_in(jax.random.fold_in(own_key, 6), axis_at), (blocks,), jnp.float32, smallest / len(cuts), largest / len(cuts))
        return jnp.repeat(jnp.exp(draws), dims[axis_at] // blocks).reshape((-1,) + (1,) * (len(dims) - axis_at - 1))

    loudness = one(*cuts[0])
    for cut in cuts[1:]:
        loudness = loudness * one(*cut)
    return loudness


def scatter_about(own_key, dims, width, most, cuts=(), kind=jnp.bfloat16):
    drawn = width * jax.random.normal(own_key, dims, jnp.float32)
    if cuts:
        drawn = drawn * steps_of(own_key, dims, cuts, -0.22, 0.18)
    return jnp.clip(drawn, -most, most).astype(kind)


def setup_inputs(seed: int = 0) -> dict:
    seeds = jax.random.split(jax.random.key(seed), 14)
    tokens = scatter_about(seeds[0], (MB, TOKENS, D), 1.0, 6.0, ((1, 8), (2, 4)))
    norm_gain = jnp.clip(1.0 + 0.1 * jax.random.normal(seeds[1], (LAYERS, D), jnp.float32), 0.5, 1.5).astype(jnp.bfloat16)
    input_weight = scatter_about(seeds[2], (LAYERS, D, 2, INNER), D ** -0.5, 0.125, ((3, 4),))
    conv_weight = scatter_about(seeds[3], (LAYERS, CONV, INNER), CONV ** -0.5, 3.0, ((2, 4),))
    conv_bias = scatter_about(seeds[4], (LAYERS, INNER), 0.5, 3.0, ((1, 4),))
    select_weight = scatter_about(seeds[5], (LAYERS, INNER, RANK + 2 * STATE), INNER ** -0.5, 0.09375, ((1, 4),))
    step_weight = scatter_about(seeds[6], (LAYERS, RANK, INNER), RANK ** -0.5, 0.5, ((2, 4),))
    step_bias = jnp.clip(-9.0 + 6.7 * jax.random.uniform(seeds[7], (LAYERS, INNER), jnp.float32) ** steps_of(seeds[7], (LAYERS, INNER), ((1, 4),), -0.2, 0.2), -9.0, -2.3)
    skip_gain = jnp.clip(1.0 + 0.1 * jax.random.normal(seeds[8], (LAYERS, INNER), jnp.float32), 0.5, 1.5).astype(jnp.bfloat16)
    out_weight = scatter_about(seeds[9], (LAYERS, INNER, D), (INNER // 8) ** -0.5, 0.25, ((1, 4),))
    cotangent = scatter_about(seeds[10], (MB, TOKENS, D), 1.0, 6.0, ((1, 8), (2, 4)))
    doc_lengths = draw_doc_lengths(jax.random.fold_in(seeds[13], 71), 0)
    doc_offsets = draw_doc_offsets(jax.random.fold_in(seeds[13], 71), 0)
    return {"tokens": tokens, "norm_gain": norm_gain, "input_weight": input_weight, "conv_weight": conv_weight, "conv_bias": conv_bias, "select_weight": select_weight, "step_weight": step_weight, "step_bias": step_bias, "skip_gain": skip_gain, "out_weight": out_weight, "cotangent": cotangent, "doc_lengths": doc_lengths, "doc_offsets": doc_offsets}


@jax.custom_vjp
def low(v):
    return lax.optimization_barrier(v.astype(jnp.bfloat16)).astype(jnp.float32)

@jax.custom_vjp
def low_back(v):
    return v

def low_keep(v):
    return (low(v), None)

def low_pass(kept, grad):
    return (grad,)

def back_keep(v):
    return (v, None)

def back_low(kept, grad):
    return (low(grad),)
low.defvjp(low_keep, low_pass)
low_back.defvjp(back_keep, back_low)
norm_epsilon = 1e-05
precision_highest = lax.Precision.HIGHEST

def gated_silu(argument):
    return argument * jax.nn.sigmoid(argument)

def block_pass(carry_pair, pieces):
    decay_total, carry_state = carry_pair
    write_rate, key_state, query_state, conv_act, keep_mask = pieces
    outputs = []
    for row in range(write_rate.shape[1]):
        key_row = key_state[:, row]
        rate_row = write_rate[:, row]
        decay = (1.0 - rate_row[:, None, :] * (key_row * key_row)[:, :, None]) * keep_mask[:, row][:, None, None]
        carry_state = decay * carry_state + (rate_row * conv_act[:, row])[:, None, :] * key_row[:, :, None]
        decay_total = decay_total * decay
        outputs.append(lax.optimization_barrier(jnp.sum(carry_state * query_state[:, row][:, :, None], axis=1)))
    return ((decay_total, carry_state), jnp.stack(outputs, axis=1))

def to_blocks(argument, block_rows):
    array_shape = argument.shape
    reshaped = argument.reshape((array_shape[0], array_shape[1] // block_rows, block_rows) + array_shape[2:])
    return jnp.moveaxis(reshaped, 1, 0)

def run_blocks(write_rate, key_state, query_state, conv_act, keep_mask, carry_state):
    block_rows = math.gcd(write_rate.shape[1], 16)
    pieces = tuple((to_blocks(member, block_rows) for member in (write_rate, key_state, query_state, conv_act, keep_mask)))
    start_pair = (jnp.ones_like(carry_state), carry_state)
    final_pair, output = lax.scan(jax.checkpoint(block_pass), start_pair, pieces)
    output = jnp.moveaxis(output, 0, 1).reshape(write_rate.shape)
    return (output, final_pair)

def mixer_layer(hidden, weights, valid_mask, keep_mask, tap_masks):
    norm_gain, input_weight, conv_weight, conv_bias, select_weight, step_weight, step_bias, skip_gain, out_weight = weights
    inverse_norm = lax.rsqrt(lax.optimization_barrier(jnp.mean(hidden * hidden, axis=1, keepdims=True)) + norm_epsilon)
    normalized_rows = low(hidden * inverse_norm * norm_gain)
    projected_rows = low_back(low(jnp.einsum('hj,jlf->hlf', normalized_rows, input_weight, precision=precision_highest)))
    conv_in = projected_rows[:, 0]
    gate_in = projected_rows[:, 1]
    edge_rows = CONV - 1
    padded = jnp.pad(conv_in, ((edge_rows, 0), (0, 0)))
    conv_out = jnp.broadcast_to(conv_bias, conv_in.shape)
    for shift_back in range(CONV):
        window = padded[edge_rows - shift_back:edge_rows - shift_back + TOKENS]
        conv_out = conv_out + conv_weight[shift_back] * window * tap_masks[shift_back][:, None]
    conv_act = low(gated_silu(conv_out))
    selection = low_back(jnp.dot(conv_act, select_weight, precision=precision_highest))
    low_rank = low(selection[:, :RANK])
    key_state = selection[:, RANK:RANK + STATE]
    query_state = selection[:, RANK + STATE:]
    pre_step = low_back(jnp.dot(low_rank, step_weight, precision=precision_highest))
    step_size = jax.nn.softplus(pre_step + step_bias)
    key_norm = lax.optimization_barrier(jnp.sum(key_state * key_state, axis=1, keepdims=True))
    write_rate = step_size / (1.0 + step_size * key_norm)
    start_state = jnp.zeros((1, STATE, INNER), jnp.float32)
    recurrent, _ = run_blocks(write_rate[None], key_state[None], query_state[None], conv_act[None], keep_mask[None], start_state)
    mixed_out = recurrent[0] + skip_gain * conv_act
    gated_out = low(mixed_out * gated_silu(gate_in))
    branch = low_back(jnp.dot(gated_out, out_weight, precision=precision_highest))
    return hidden + valid_mask[:, None] * branch

def micro_batch(tokens_row, lengths_row, offsets_row, weights):
    positions = jnp.arange(TOKENS).astype(jnp.int32)
    before = offsets_row[None, :] <= positions[:, None]
    starts = lax.optimization_barrier(jnp.max(jnp.where(before, offsets_row[None, :], 0), axis=1))
    doc_ends = lax.optimization_barrier(jnp.max(jnp.where(before, offsets_row[None, :] + lengths_row[None, :], 0), axis=1))
    valid_mask = (positions < doc_ends).astype(jnp.float32)
    keep_mask = (positions != starts).astype(jnp.float32)
    tap_masks = [(positions - shift_back >= starts).astype(jnp.float32) for shift_back in range(CONV)]
    hidden = tokens_row
    for layer_index in range(LAYERS):
        layer_weights = tuple((member[layer_index] for member in weights))
        hidden = jax.checkpoint(mixer_layer)(hidden, layer_weights, valid_mask, keep_mask, tap_masks)
    return hidden

def forward(tokens, weights, doc_lengths, doc_offsets):

    def one_batch(member):
        return micro_batch(member[0], member[1], member[2], weights)
    return lax.map(jax.checkpoint(one_batch), (tokens, doc_lengths, doc_offsets))

def reference(tokens, norm_gain, input_weight, conv_weight, conv_bias, select_weight, step_weight, step_bias, skip_gain, out_weight, cotangent, doc_lengths, doc_offsets):
    floats = tuple((member.astype(jnp.float32) for member in (tokens, norm_gain, input_weight, conv_weight, conv_bias, select_weight, step_weight, step_bias, skip_gain, out_weight)))

    def apply_all(*members):
        return forward(members[0], members[1:], doc_lengths, doc_offsets)
    result, pullback = jax.vjp(apply_all, *floats)
    grads = pullback(cotangent.astype(jnp.float32))
    select_full = grads[5]
    return (result.astype(jnp.bfloat16), grads[0].astype(jnp.bfloat16), grads[1], grads[2], grads[3], grads[4], select_full[:, :, :RANK], select_full[:, :, RANK:], grads[6], grads[7], grads[8], grads[9])
```

```python
import functools
import jax
import jax.numpy as jnp
import numpy as np
from jax import lax
from jax.experimental import pallas as pl
from jax.experimental.pallas import tpu as pltpu
from jax.sharding import PartitionSpec as P

CH = 16
LANES = 128
VMEM_BYTES = 40 * 1024 * 1024
norm_epsilon = 1e-05
BLOCK = 128
F32 = jnp.float32
LOW = jnp.bfloat16


def tables(states):
    wide = CH * states
    rows = np.arange(wide)
    lanes = np.arange(LANES)
    repeat = (rows[:, None] // states == np.arange(CH)[None, :]).astype(np.float32)
    picks = [lanes[:, None] == group * states + rows[None, :] % states for group in (0, 1, 3)]
    diagonal = (np.arange(CH)[:, None] == rows[None, :] // states).astype(np.float32)
    fold = (np.arange(3 * LANES)[:, None] // LANES == lanes[None, :] // states).astype(np.float32)
    fold_own = (rows[:, None] % states == lanes[None, :] % states).astype(np.float32)
    low = lambda value: jnp.asarray(value, LOW)
    return dict(
        pick=low(np.stack(picks).astype(np.float32)),
        diagonal=jnp.asarray(diagonal, F32),
        fold=low(fold),
        fold_own=jnp.asarray(fold_own, F32),
        gather=low(repeat.T),
    )


def dot(left, right):
    return jnp.dot(left, right, preferred_element_type=F32)


def spread_rows(table, row, states):
    wide = jnp.broadcast_to(table[:, row : row + 1], (table.shape[0], LANES))
    return [wide[at : at + states] for at in range(0, 4 * states, states)]


def groups(width):
    return [slice(at, at + LANES) for at in range(0, width, LANES)]


def row_of(ref, at, lanes):
    return ref[at : at + 1, lanes]


def summary_kernel(
    states, r_ref, act_ref, col_ref, out_ref, *scratch
):
    feed_refs = scratch[0:2]
    decay_ref, state_ref = scratch[2:]
    step = pl.program_id(1)
    r_ref, act_ref, col_ref = r_ref.at[0], act_ref.at[0], col_ref.at[0]
    count = r_ref.shape[0] // CH
    parts = groups(r_ref.shape[1])

    @pl.when(step == 0)
    def _():
        decay_ref[...] = jnp.ones_like(decay_ref)
        state_ref[...] = jnp.zeros_like(state_ref)

    def prepare(index, which):
        rows = pl.ds(pl.multiple_of(index * CH, CH), CH)
        feed_refs[which][...] = r_ref[rows, :] * act_ref[rows, :].astype(F32)

    def process(index, which, decays, values):
        base = pl.multiple_of(index * CH, CH)
        rates = r_ref.at[pl.ds(base, CH)]
        table, feeds = col_ref[pl.ds(base, CH), :].T[: 4 * states], feed_refs[which]
        for row in range(CH):
            mine = slice(row * states, (row + 1) * states)
            key, square, keep, _ = spread_rows(table, row, states)
            for at, lanes in enumerate(parts):
                decay = keep - row_of(rates, row, lanes) * square
                values[at] = decay * values[at] + row_of(feeds, row, lanes) * key
                decays[at] = decays[at] * decay

    prepare(0, 0)

    def pair(turn, carry):
        decays, values = list(carry[0]), list(carry[1])
        prepare(2 * turn + 1, 1)
        process(2 * turn, 0, decays, values)
        prepare(jnp.minimum(2 * turn + 2, count - 1), 0)
        process(2 * turn + 1, 1, decays, values)
        return (tuple(decays), tuple(values))

    start = (
        tuple(decay_ref[:, lanes] for lanes in parts),
        tuple(state_ref[:, lanes] for lanes in parts),
    )
    decays, values = lax.fori_loop(0, count // 2, pair, start)
    for at, lanes in enumerate(parts):
        decay_ref[:, lanes] = decays[at]
        state_ref[:, lanes] = values[at]

    @pl.when(step == pl.num_programs(1) - 1)
    def _():
        out_ref[0, :states] = decay_ref[...].astype(out_ref.dtype)
        out_ref[0, states:] = state_ref[...].astype(out_ref.dtype)


def forward_kernel(
    states,
    r_ref,
    act_ref,
    col_ref,
    gate_ref,
    skip_ref,
    in_ref,
    pick_ref,
    diagonal_ref,
    states_ref,
    mixed_ref,
    gated_ref,
    *scratch,
):
    feed_refs, value_refs, (state_ref,) = scratch[0:2], scratch[2:4], scratch[4:]
    step = pl.program_id(1)
    r_ref, act_ref, col_ref, gate_ref = r_ref.at[0], act_ref.at[0], col_ref.at[0], gate_ref.at[0]
    states_ref, mixed_ref, gated_ref = states_ref.at[0], mixed_ref.at[0], gated_ref.at[0]
    count = r_ref.shape[0] // CH
    parts = groups(r_ref.shape[1])

    @pl.when(step == 0)
    def _():
        state_ref[...] = in_ref[0].astype(F32)

    def prepare(index, which):
        rows = pl.ds(pl.multiple_of(index * CH, CH), CH)
        feed_refs[which][...] = r_ref[rows, :] * act_ref[rows, :].astype(F32)

    def process(index, which, values):
        base = pl.multiple_of(index * CH, CH)
        rates = r_ref.at[pl.ds(base, CH)]
        first = pl.multiple_of(index * (CH * states), CH * states)
        table, feeds = col_ref[pl.ds(base, CH), :].T[: 4 * states], feed_refs[which]
        for row in range(CH):
            mine = slice(row * states, (row + 1) * states)
            key, square, keep, _ = spread_rows(table, row, states)
            for at, lanes in enumerate(parts):
                decay = keep - row_of(rates, row, lanes) * square
                values[at] = decay * values[at] + row_of(feeds, row, lanes) * key
                low = values[at].astype(LOW)
                states_ref[pl.ds(first + row * states, states), lanes] = low
                value_refs[which][mine, lanes] = low

    def finish(index, which):
        rows = pl.ds(pl.multiple_of(index * CH, CH), CH)
        query = (dot(col_ref[rows, :].astype(LOW), pick_ref[2]) * diagonal_ref[...]).astype(LOW)
        recurrent = dot(query, value_refs[which][...])
        mixed = recurrent + skip_ref[...] * act_ref[rows, :].astype(F32)
        gate = gate_ref[rows, :].astype(F32)
        mixed_ref[rows, :] = mixed.astype(mixed_ref.dtype)
        gated_ref[rows, :] = (mixed * gate / (1.0 + jnp.exp(-gate))).astype(gated_ref.dtype)

    prepare(0, 0)

    def pair(turn, carry):
        values = list(carry)
        prepare(2 * turn + 1, 1)
        process(2 * turn, 0, values)
        finish(2 * turn, 0)
        prepare(jnp.minimum(2 * turn + 2, count - 1), 0)
        process(2 * turn + 1, 1, values)
        finish(2 * turn + 1, 1)
        return tuple(values)

    values = lax.fori_loop(0, count // 2, pair, tuple(state_ref[:, lanes] for lanes in parts))
    for at, lanes in enumerate(parts):
        state_ref[:, lanes] = values[at]


def adjoint_kernel(
    states, r_ref, gm_ref, col_ref, out_ref, *scratch
):
    (carry_ref,) = scratch
    step = pl.program_id(1)
    r_ref, gm_ref, col_ref = r_ref.at[0], gm_ref.at[0], col_ref.at[0]
    count = r_ref.shape[0] // CH
    parts = groups(r_ref.shape[1])

    @pl.when(step == 0)
    def _():
        carry_ref[...] = jnp.zeros_like(carry_ref)


    def process(index, which, values):
        base = pl.multiple_of(index * CH, CH)
        rates = r_ref.at[pl.ds(base, CH)]
        grads = gm_ref.at[pl.ds(base, CH)]
        table = col_ref[pl.ds(base, CH), :].T[: 4 * states]
        for row in reversed(range(CH)):
            mine = slice(row * states, (row + 1) * states)
            _, square, keep, query = spread_rows(table, row, states)
            for at, lanes in enumerate(parts):
                adjoint = query * row_of(grads, row, lanes) + values[at]
                values[at] = (keep - row_of(rates, row, lanes) * square) * adjoint


    def pair(turn, carry):
        values = list(carry)
        index = count - 1 - 2 * turn
        process(index, 0, values)
        process(index - 1, 1, values)
        return tuple(values)

    values = lax.fori_loop(0, count // 2, pair, tuple(carry_ref[:, lanes] for lanes in parts))
    for at, lanes in enumerate(parts):
        carry_ref[:, lanes] = values[at]

    @pl.when(step == pl.num_programs(1) - 1)
    def _():
        out_ref[0] = carry_ref[...].astype(out_ref.dtype)


def backward_kernel(
    states,
    r_ref,
    act_ref,
    gm_ref,
    col_ref,
    skip_ref,
    states_ref,
    before_ref,
    in_ref,
    carry_in_ref,
    pick_ref,
    diagonal_ref,
    fold_ref,
    fold_own_ref,
    gather_ref,
    rate_ref,
    gact_ref,
    sums_ref,
    *scratch,
):
    feed_refs, adjoint_refs, product_refs, part_refs = (
        scratch[2 * at : 2 * at + 2] for at in range(4)
    )
    first_ref, carry_ref = scratch[8:]
    step = pl.program_id(1)
    last = pl.num_programs(1) - 1
    r_ref, act_ref, gm_ref, col_ref = r_ref.at[0], act_ref.at[0], gm_ref.at[0], col_ref.at[0]
    states_ref, rate_ref, gact_ref, sums_ref = (
        states_ref.at[0],
        rate_ref.at[0],
        gact_ref.at[0],
        sums_ref.at[0],
    )
    count = r_ref.shape[0] // CH
    parts = groups(r_ref.shape[1])

    @pl.when(step == 0)
    def _():
        carry_ref[...] = carry_in_ref[0].astype(F32)

    @pl.when(step == last)
    def _():
        first_ref[...] = in_ref[0].astype(LOW)

    @pl.when(step != last)
    def _():
        first_ref[...] = before_ref[0]

    def prepare(index, which):
        rows = pl.ds(pl.multiple_of(index * CH, CH), CH)
        feed_refs[which][...] = r_ref[rows, :] * act_ref[rows, :].astype(F32)

    def process(index, which, values, held):
        base = pl.multiple_of(index * CH, CH)
        rates = r_ref.at[pl.ds(base, CH)]
        grads = gm_ref.at[pl.ds(base, CH)]
        first = pl.multiple_of(index * (CH * states), CH * states)
        table, feeds = col_ref[pl.ds(base, CH), :].T[: 4 * states], feed_refs[which]
        for row in reversed(range(CH)):
            mine = slice(row * states, (row + 1) * states)
            _, square, keep, query = spread_rows(table, row, states)
            sums = [None, None, None]
            for at, lanes in enumerate(parts):
                rate = row_of(rates, row, lanes)
                grad = row_of(grads, row, lanes)
                if row:
                    previous = states_ref[pl.ds(first + (row - 1) * states, states), lanes]
                else:
                    before = pl.multiple_of(jnp.maximum(first - states, 0), states)
                    previous = jnp.where(
                        index == 0, first_ref[:, lanes], states_ref[pl.ds(before, states), lanes]
                    )
                previous = previous.astype(F32)
                adjoint = query * grad + values[at]
                product = adjoint * previous
                values[at] = (keep - rate * square) * adjoint
                adjoint_refs[which][mine, lanes] = adjoint.astype(LOW)
                product_refs[which][mine, lanes] = product.astype(LOW)
                terms = (adjoint * row_of(feeds, row, lanes), product * rate, held[at] * grad)
                for kind, term in enumerate(terms):
                    sums[kind] = term if sums[kind] is None else sums[kind] + term
                held[at] = previous
            for kind in range(3):
                part_refs[which][mine, kind * LANES : (kind + 1) * LANES] = sums[kind].astype(LOW)

    def finish(index, which):
        rows = pl.ds(pl.multiple_of(index * CH, CH), CH)
        cols = col_ref[rows, :].astype(LOW)
        keys = (dot(cols, pick_ref[0]) * diagonal_ref[...]).astype(LOW)
        squares = (dot(cols, pick_ref[1]) * diagonal_ref[...]).astype(LOW)
        through_key = dot(keys, adjoint_refs[which][...])
        through_decay = dot(squares, product_refs[which][...])
        rate_ref[rows, :] = act_ref[rows, :].astype(F32) * through_key - through_decay
        gact_ref[rows, :] = r_ref[rows, :] * through_key + skip_ref[...] * gm_ref[rows, :]
        folded = dot(part_refs[which][...], fold_ref[...]) * fold_own_ref[...]
        high = folded.astype(LOW)
        rest = (folded - high.astype(F32)).astype(LOW)
        sums_ref[rows, :] = dot(gather_ref[...], high) + dot(gather_ref[...], rest)

    prepare(count - 1, 0)

    def pair(turn, carry):
        values, held = list(carry[0]), list(carry[1])
        index = count - 1 - 2 * turn
        prepare(index - 1, 1)
        process(index, 0, values, held)
        finish(index, 0)
        prepare(jnp.maximum(index - 2, 0), 0)
        process(index - 1, 1, values, held)
        finish(index - 1, 1)
        return (tuple(values), tuple(held))

    tail = pl.ds((count * CH - 1) * states, states)
    start = (
        tuple(carry_ref[:, lanes] for lanes in parts),
        tuple(states_ref[tail, lanes].astype(F32) for lanes in parts),
    )
    values, _ = lax.fori_loop(0, count // 2, pair, start)
    for at, lanes in enumerate(parts):
        carry_ref[:, lanes] = values[at]


def plan(rate):
    batch, rows, channels = rate.shape
    block = 128 if rows % 128 == 0 else rows
    return batch, rows, channels, block, (batch, rows // block)


def cost(rate, states, work):
    size = rate.shape[0] * rate.shape[1] * rate.shape[2] * states
    return pl.CostEstimate(flops=size * work, bytes_accessed=size * 2, transcendentals=0)


def params():
    return pltpu.CompilerParams(
        dimension_semantics=("arbitrary", "arbitrary"), vmem_limit_bytes=VMEM_BYTES
    )


def whole(value):
    return pl.BlockSpec(value.shape, lambda m, b: (0,) * value.ndim)


def run_summary(rate, act, cols, states):
    batch, rows, channels, block, grid = plan(rate)
    part = pl.BlockSpec((1, block, channels), lambda m, b: (m, b, 0))
    narrow = pl.BlockSpec((1, block, LANES), lambda m, b: (m, b, 0))
    return pl.pallas_call(
        functools.partial(summary_kernel, states),
        grid=grid,
        in_specs=[part, part, narrow],
        out_specs=pl.BlockSpec((1, 2 * states, channels), lambda m, b: (m, 0, 0)),
        out_shape=jax.ShapeDtypeStruct((batch, 2 * states, channels), LOW),
        scratch_shapes=[pltpu.VMEM((CH, channels), F32)] * 2
        + [pltpu.VMEM((states, channels), F32)] * 2,
        compiler_params=params(),
        cost_estimate=cost(rate, states, 6),
    )(rate, act, cols)


def run_forward(rate, act, cols, gate, skip, incoming, states, table):
    batch, rows, channels, block, grid = plan(rate)
    part = pl.BlockSpec((1, block, channels), lambda m, b: (m, b, 0))
    narrow = pl.BlockSpec((1, block, LANES), lambda m, b: (m, b, 0))
    edge = pl.BlockSpec((1, states, channels), lambda m, b: (m, 0, 0))
    consts = [table[name] for name in ("pick", "diagonal")]
    return pl.pallas_call(
        functools.partial(forward_kernel, states),
        grid=grid,
        in_specs=[part, part, narrow, part, whole(skip), edge] + [whole(value) for value in consts],
        out_specs=[
            pl.BlockSpec((1, block * states, channels), lambda m, b: (m, b, 0)),
            part,
            part,
        ],
        out_shape=[
            jax.ShapeDtypeStruct((batch, rows * states, channels), LOW),
            jax.ShapeDtypeStruct((batch, rows, channels), LOW),
            jax.ShapeDtypeStruct((batch, rows, channels), LOW),
        ],
        scratch_shapes=[pltpu.VMEM((CH, channels), F32)] * 2
        + [pltpu.VMEM((CH * states, channels), LOW)] * 2
        + [pltpu.VMEM((states, channels), F32)],
        compiler_params=params(),
        cost_estimate=cost(rate, states, 8),
    )(rate, act, cols, gate, skip, incoming, *consts)


def run_adjoint(rate, grad_mixed, cols, states):
    batch, rows, channels, block, grid = plan(rate)
    final = rows // block - 1
    part = pl.BlockSpec((1, block, channels), lambda m, b: (m, final - b, 0))
    narrow = pl.BlockSpec((1, block, LANES), lambda m, b: (m, final - b, 0))
    return pl.pallas_call(
        functools.partial(adjoint_kernel, states),
        grid=grid,
        in_specs=[part, part, narrow],
        out_specs=pl.BlockSpec((1, states, channels), lambda m, b: (m, 0, 0)),
        out_shape=jax.ShapeDtypeStruct((batch, states, channels), LOW),
        scratch_shapes=[pltpu.VMEM((states, channels), F32)],
        compiler_params=params(),
        cost_estimate=cost(rate, states, 5),
    )(rate, grad_mixed, cols)


def run_backward(rate, act, grad_mixed, cols, skip, kept_states, incoming, carry, states, table):
    batch, rows, channels, block, grid = plan(rate)
    final = rows // block - 1
    part = pl.BlockSpec((1, block, channels), lambda m, b: (m, final - b, 0))
    narrow = pl.BlockSpec((1, block, LANES), lambda m, b: (m, final - b, 0))
    edge = pl.BlockSpec((1, states, channels), lambda m, b: (m, 0, 0))
    names = ("pick", "diagonal", "fold", "fold_own", "gather")
    consts = [table[name] for name in names]
    return pl.pallas_call(
        functools.partial(backward_kernel, states),
        grid=grid,
        in_specs=[
            part,
            part,
            part,
            narrow,
            whole(skip),
            pl.BlockSpec((1, block * states, channels), lambda m, b: (m, final - b, 0)),
            pl.BlockSpec(
                (1, states, channels),
                lambda m, b: (m, jnp.maximum((final - b) * block - 1, 0), 0),
            ),
            edge,
            edge,
        ]
        + [whole(value) for value in consts],
        out_specs=[part, part, narrow],
        out_shape=[
            jax.ShapeDtypeStruct((batch, rows, channels), F32),
            jax.ShapeDtypeStruct((batch, rows, channels), F32),
            jax.ShapeDtypeStruct((batch, rows, LANES), F32),
        ],
        scratch_shapes=[pltpu.VMEM((CH, channels), F32)] * 2
        + [pltpu.VMEM((CH * states, channels), LOW)] * 4
        + [pltpu.VMEM((CH * states, 3 * LANES), LOW)] * 2
        + [pltpu.VMEM((states, channels), LOW), pltpu.VMEM((states, channels), F32)],
        compiler_params=params(),
        cost_estimate=cost(rate, states, 16),
    )(rate, act, grad_mixed, cols, skip, kept_states, kept_states, incoming, carry, *consts)


def columns(key, query, keep):
    kept = jnp.broadcast_to(keep[:, :, None], key.shape)
    parts = [key, kept * key * key, kept, query]
    blank = jnp.zeros(key.shape[:2] + (LANES - 4 * key.shape[2],), F32)
    return jnp.concatenate(parts + [blank], axis=2)


def shifted(value, axis, steps):
    count = lax.axis_size(axis)
    leading, last = (max(0, -steps), min(count, count - steps))
    return lax.ppermute(value, axis, [(source, source + steps) for source in range(leading, last)])


def swapped(value, axis, bit):
    count = lax.axis_size(axis)
    return lax.ppermute(value, axis, [(source, source ^ bit) for source in range(count)])


def odd(axis, bit):
    return (lax.axis_index(axis) // bit) % 2 == 1


def tp_bits():
    count = lax.axis_size("tp")
    return [1 << at for at in range(count.bit_length() - 1)]


def tp_sum(value, kind):
    for bit in tp_bits():
        value = value + swapped(value.astype(kind), "tp", bit).astype(F32)
    return value


def tp_gather(value):
    pieces = {0: value}
    for bit in reversed(tp_bits()):
        for at in list(pieces):
            pieces[at + bit] = swapped(pieces[at], "tp", bit)
    ordered = [pieces[at] for at in range(len(pieces))]
    for bit in tp_bits():
        flip = odd("tp", bit)
        ordered = [
            jnp.where(flip, ordered[at ^ bit], ordered[at]) for at in range(len(ordered))
        ]
    return jnp.concatenate(ordered, axis=-1)


def tp_scatter(value):
    count = lax.axis_size("tp")
    width = value.shape[-1] // count
    parts = [value[..., at * width : (at + 1) * width] for at in range(count)]
    for bit in tp_bits():
        flip = odd("tp", bit)
        pairs = [(parts[2 * at], parts[2 * at + 1]) for at in range(len(parts) // 2)]
        sent = [jnp.where(flip, even, other).astype(LOW) for even, other in pairs]
        mine = [jnp.where(flip, other, even) for even, other in pairs]
        parts = [
            here + swapped(there, "tp", bit).astype(F32) for here, there in zip(mine, sent)
        ]
    return parts[0]


def scan_exclusive(decay, value, direction):
    count = lax.axis_size("seq")
    states = decay.shape[1]
    outer = None
    step = 1
    while step < count:
        packed = jnp.concatenate([decay, value], axis=1).astype(LOW)
        final = 2 * step >= count
        got = shifted(packed[:, states:] if final else packed, "seq", direction * step).astype(F32)
        if final:
            got_value = got
        else:
            got_decay, got_value = got[:, :states], got[:, states:]
        if outer is None:
            outer = (got_decay, got_value) if not final else (None, got_value)
        else:
            total, held = outer
            outer = (None if final else total * got_decay, total * got_value + held)
        if not final:
            value = decay * got_value + value
            decay = decay * got_decay
        step *= 2
    return outer[1]


def halves(value):
    count = lax.axis_size("seq")
    batch, rows, width = value.shape
    parted = value.reshape(batch, rows, count // 2, 2, width // count)
    even, other = (
        parted[:, :, :, at, :].reshape(batch * rows, width // 2) for at in range(2)
    )
    flip = odd("seq", 1)
    mine = jnp.where(flip, other, even)
    theirs = swapped(jnp.where(flip, even, other), "seq", 1)
    return jnp.concatenate([mine, theirs], axis=0)


def paired(value):
    flat = value.reshape(-1, value.shape[-1])
    return jnp.concatenate([flat, swapped(flat, "seq", 1)], axis=0)


def line_reduce(value):
    long = lax.axis_size("seq") // 2
    place = lax.axis_index("seq") // 2
    pairs = lambda sources, move: [
        (2 * source + side, 2 * (source + move) + side) for source in sources for side in range(2)
    ]
    pick = lambda at: lax.dynamic_index_in_dim(value, jnp.clip(at, 0, long - 1), 0, False)
    right, left = None, None
    for step in range(1, long):
        ahead = pick(place + long - step)
        behind = pick(place - long + step)
        if right is not None:
            ahead = (ahead.astype(F32) + right.astype(F32)).astype(LOW)
            behind = (behind.astype(F32) + left.astype(F32)).astype(LOW)
        right = lax.ppermute(ahead, "seq", pairs(range(min(step, long - 1)), 1))
        left = lax.ppermute(behind, "seq", pairs(range(max(long - step, 1), long), -1))
    own = pick(place).astype(F32)
    if right is not None:
        own = own + right.astype(F32) + left.astype(F32)
    return own


def seq_scatter(value):
    count = lax.axis_size("seq")
    bit = count // 2
    while bit:
        flip = odd("seq", bit)
        low, high = value[: value.shape[0] // 2], value[value.shape[0] // 2 :]
        sent = jnp.where(flip, low, high).astype(LOW)
        value = jnp.where(flip, high, low).astype(F32) + swapped(sent, "seq", bit).astype(F32)
        bit //= 2
    return value


def seq_sum(value):
    count = lax.axis_size("seq")
    bit = 1
    while bit < count:
        value = value + swapped(value.astype(LOW), "seq", bit).astype(F32)
        bit *= 2
    return value


def gated_silu(argument):
    return argument * jax.nn.sigmoid(argument)


def silu_slope(argument):
    logistic = jax.nn.sigmoid(argument)
    return logistic * (1.0 + argument * (1.0 - logistic))


def doc_masks(doc_lengths, doc_offsets, positions):
    before = doc_offsets[:, None, :] <= positions[None, :, None]
    starts = jnp.max(jnp.where(before, doc_offsets[:, None, :], 0), axis=2)
    doc_ends = jnp.max(
        jnp.where(before, doc_offsets[:, None, :] + doc_lengths[:, None, :], 0), axis=2
    )
    return (starts, (positions[None, :] < doc_ends).astype(F32))


def matmul(left, right, dims):
    return jnp.einsum(dims, left, right, preferred_element_type=F32)


def conv_forward(conv_in, previous, conv_weight, conv_bias, tap_masks):
    edge = conv_weight.shape[0] - 1
    rows = conv_in.shape[1]
    extended = jnp.concatenate([previous, conv_in], axis=1).astype(F32)
    running = conv_bias.astype(F32)
    for back in range(edge + 1):
        window = extended[:, edge - back : edge - back + rows]
        running = running + conv_weight[back].astype(F32) * window * tap_masks[back][:, :, None]
    return (extended, running)


def forward_layer(hidden, weights, valid_mask, keep_mask, tap_masks, table):
    gain, conv_w, gate_w, conv_weight, conv_bias, select_w, step_w, step_bias, skip, out_w = weights
    width = conv_w.shape[0]
    scaled = (hidden * gain.astype(F32)).astype(LOW)
    square_sums = tp_sum(jnp.sum(hidden * hidden, axis=2), F32)
    inverse_norm = lax.rsqrt(square_sums / width + norm_epsilon)
    complete = tp_gather(scaled)
    conv_in = (matmul(complete, conv_w, "bph,hg->bpg") * inverse_norm[:, :, None]).astype(LOW)
    edge = conv_weight.shape[0] - 1
    rows = hidden.shape[1]
    previous = shifted(conv_in[:, rows - edge :], "seq", 1)
    extended, conv_out = conv_forward(conv_in, previous, conv_weight, conv_bias, tap_masks)
    conv_act = gated_silu(conv_out).astype(LOW)
    selection = tp_sum(matmul(conv_act, select_w, "mri,ic->mrc"), LOW)
    gate_in = (matmul(complete, gate_w, "bph,hg->bpg") * inverse_norm[:, :, None]).astype(LOW)
    rank = step_w.shape[0]
    states = (selection.shape[2] - rank) // 2
    low_rank = selection[:, :, :rank].astype(LOW)
    key_state = selection[:, :, rank : rank + states]
    query_state = selection[:, :, rank + states :]
    biased = matmul(low_rank, step_w, "mrk,ki->mri") + step_bias
    step_size = jax.nn.softplus(biased)
    key_norm = jnp.sum(key_state * key_state, axis=2)
    rate = step_size / (1.0 + step_size * key_norm[:, :, None])
    cols = columns(key_state, query_state, keep_mask)
    summary = run_summary(rate, conv_act, cols, states).astype(F32)
    decay_total, local_state = summary[:, :states], summary[:, states:]
    incoming = scan_exclusive(decay_total, local_state, 1)
    skip_row = skip.astype(F32)[None]
    kept_states, mixed, gated = run_forward(
        rate, conv_act, cols, gate_in, skip_row, incoming, states, table
    )
    branch = tp_scatter(matmul(gated, out_w, "mri,id->mrd"))
    new_hidden = hidden + valid_mask[:, :, None] * branch
    kept = dict(
        hidden=hidden,
        inverse_norm=inverse_norm,
        complete=complete,
        conv_in=conv_in,
        gate_in=gate_in,
        extended=extended,
        conv_out=conv_out,
        conv_act=conv_act,
        low_rank=low_rank,
        key_state=key_state,
        cols=cols,
        biased=biased,
        key_norm=key_norm,
        rate=rate,
        decay_total=decay_total,
        incoming=incoming,
        kept_states=kept_states,
        mixed=mixed,
        gated=gated,
    )
    return (new_hidden, kept)


def backward_layer(grad_new, weights, kept, valid_mask, keep_mask, tap_masks, table):
    gain, conv_w, gate_w, conv_weight, conv_bias, select_w, step_w, step_bias, skip, out_w = weights
    hidden, inverse_norm, rate, cols = (
        kept[name] for name in ("hidden", "inverse_norm", "rate", "cols")
    )
    conv_act, key_state = kept["conv_act"], kept["key_state"]
    width = conv_w.shape[0]
    states = key_state.shape[2]
    rank = step_w.shape[0]
    long = lax.axis_size("seq") // 2
    skip_row = skip.astype(F32)[None]
    branch_rows = tp_gather((grad_new * valid_mask[:, :, None]).astype(LOW))
    grad_gated = matmul(branch_rows, out_w, "mrd,id->mri")
    gate_in = kept["gate_in"].astype(F32)
    grad_mixed = grad_gated * gated_silu(gate_in)
    grad_gate = grad_gated * kept["mixed"].astype(F32) * silu_slope(gate_in)
    act_float = conv_act.astype(F32)
    skip_grad = jnp.sum(grad_mixed * act_float, axis=(0, 1))
    local_carry = run_adjoint(rate, grad_mixed, cols, states).astype(F32)
    carried = scan_exclusive(kept["decay_total"], local_carry, -1)
    grad_rate, grad_act, sums = run_backward(
        rate,
        conv_act,
        grad_mixed,
        cols,
        skip_row,
        kept["kept_states"],
        kept["incoming"],
        carried,
        states,
        table,
    )
    branch_half = halves(branch_rows)
    outweight_grad = matmul(branch_half, paired(kept["gated"]), "rd,ri->di").astype(LOW)
    outweight_grad = line_reduce(outweight_grad.reshape(long, -1, outweight_grad.shape[1]))
    normed_half = halves(kept["complete"])
    inverse = inverse_norm[:, :, None]
    grad_gate = (grad_gate * inverse).astype(LOW)
    gate_grad = matmul(normed_half, paired(grad_gate), "rd,ri->di").astype(LOW)
    gate_grad = line_reduce(gate_grad.reshape(long, -1, gate_grad.shape[1]))
    denominator = 1.0 + jax.nn.softplus(kept["biased"]) * kept["key_norm"][:, :, None]
    grad_step = grad_rate / (denominator * denominator)
    grad_norm_key = -jnp.sum(grad_rate * rate * rate, axis=2)
    grad_pre = grad_step * jax.nn.sigmoid(kept["biased"])
    stepbias_grad = jnp.sum(grad_pre, axis=(0, 1))
    grad_pre_low = grad_pre.astype(LOW)
    step_grad = matmul(kept["low_rank"], grad_pre_low, "mrk,mri->ki")
    grad_rank = matmul(grad_pre_low, step_w, "mri,ki->mrk")
    through_feed, through_decay, grad_query = (
        sums[:, :, at * states : (at + 1) * states] for at in range(3)
    )
    grad_key = (
        through_feed
        - 2.0 * keep_mask[:, :, None] * key_state * through_decay
        + 2.0 * key_state * grad_norm_key[:, :, None]
    )
    grad_selection = tp_sum(jnp.concatenate([grad_rank, grad_key, grad_query], axis=2), LOW)
    grad_selection = grad_selection.astype(LOW)
    select_full = matmul(grad_selection, conv_act, "mrc,mri->ci")
    grad_act = grad_act + matmul(grad_selection, select_w, "mrc,ic->mri")
    grad_conv = grad_act * silu_slope(kept["conv_out"])
    convbias_grad = jnp.sum(grad_conv, axis=(0, 1))
    edge = conv_weight.shape[0] - 1
    rows = grad_conv.shape[1]
    extended = kept["extended"]
    tap_grads = []
    grad_extended = jnp.zeros(extended.shape, F32)
    for back in range(edge + 1):
        masked = grad_conv * tap_masks[back][:, :, None]
        tap_grads.append(jnp.sum(masked * extended[:, edge - back : edge - back + rows], axis=(0, 1)))
        grad_extended = grad_extended + jnp.pad(
            masked * conv_weight[back].astype(F32), ((0, 0), (edge - back, back), (0, 0))
        )
    returned = shifted(grad_extended[:, :edge], "seq", -1)
    grad_conv_in = grad_extended[:, edge:] + jnp.pad(
        returned, ((0, 0), (rows - edge, 0), (0, 0))
    )
    grad_conv_in = (grad_conv_in * inverse).astype(LOW)
    grad_normed = matmul(grad_conv_in, conv_w, "bpg,hg->bph") + matmul(
        grad_gate, gate_w, "bpg,hg->bph"
    )
    grad_normed = tp_scatter(grad_normed)
    inner = tp_sum(
        jnp.sum(
            grad_conv_in.astype(F32) * kept["conv_in"].astype(F32)
            + grad_gate.astype(F32) * gate_in,
            axis=2,
        ),
        F32,
    )
    conv_grad = matmul(normed_half, paired(grad_conv_in), "rd,ri->di").astype(LOW)
    conv_grad = line_reduce(conv_grad.reshape(long, -1, conv_grad.shape[1]))
    gain_grad = jnp.sum(grad_normed * hidden, axis=(0, 1))
    grad_hidden = (
        grad_new
        + gain.astype(F32) * grad_normed
        - hidden * (inverse_norm * inner / width)[:, :, None]
    )
    count = lax.axis_size("seq")
    scattered = jnp.stack([select_full[:rank], step_grad], axis=0)
    scattered = scattered.reshape(2, count, rank // count, -1).swapaxes(0, 1)
    scattered = seq_scatter(scattered)[0]
    channels = conv_act.shape[2]
    summed = seq_sum(
        jnp.concatenate(
            [
                jnp.stack(tap_grads + [convbias_grad, stepbias_grad, skip_grad], axis=0),
                select_full[rank:],
                jnp.pad(gain_grad, (0, channels - gain_grad.shape[0]))[None],
            ],
            axis=0,
        )
    )
    grads = dict(
        inweight=jnp.stack([conv_grad, gate_grad], axis=1),
        outweight=outweight_grad.T,
        select=scattered[0].T,
        step=scattered[1],
        convweight=summed[: edge + 1],
        convbias=summed[edge + 1],
        stepbias=summed[edge + 2],
        skip=summed[edge + 3],
        keyquery=summed[edge + 4 : -1].T,
        gain=summed[-1, : gain_grad.shape[0]],
    )
    return (grad_hidden, grads)


def on_device(
    tokens,
    norm_gain,
    input_weight,
    conv_weight,
    conv_bias,
    select_weight,
    step_weight,
    step_bias,
    skip_gain,
    out_weight,
    cotangent,
    doc_lengths,
    doc_offsets,
):
    rows = tokens.shape[1]
    positions = lax.axis_index("seq") * rows + jnp.arange(rows, dtype=jnp.int32)
    starts, valid_mask = doc_masks(doc_lengths, doc_offsets, positions)
    keep_mask = (positions[None, :] != starts).astype(F32)
    tap_masks = [
        (positions[None, :] - back >= starts).astype(F32) for back in range(conv_weight.shape[1])
    ]
    layers = input_weight.shape[0]
    table = tables((select_weight.shape[2] - step_weight.shape[1]) // 2)
    weights = [
        (
            norm_gain[at],
            input_weight[at, :, 0],
            input_weight[at, :, 1],
            conv_weight[at],
            conv_bias[at],
            select_weight[at],
            step_weight[at],
            step_bias[at],
            skip_gain[at],
            out_weight[at],
        )
        for at in range(layers)
    ]
    hidden = tokens.astype(F32)
    saved = []
    for at in range(layers):
        hidden, kept = forward_layer(
            hidden, weights[at], valid_mask, keep_mask, tap_masks, table
        )
        saved.append(kept)
    layer_out = hidden.astype(LOW)
    grad = cotangent.astype(F32)
    grads = [None] * layers
    for at in reversed(range(layers)):
        grad, grads[at] = backward_layer(
            grad, weights[at], saved[at], valid_mask, keep_mask, tap_masks, table
        )
    stacked = lambda name: jnp.stack([member[name] for member in grads], axis=0)
    return (
        layer_out,
        grad.astype(LOW),
        stacked("gain"),
        stacked("inweight"),
        stacked("convweight"),
        stacked("convbias"),
        stacked("select"),
        stacked("keyquery"),
        stacked("step"),
        stacked("stepbias"),
        stacked("skip"),
        stacked("outweight"),
    )


def solution(mesh):
    placed = (
        P(None, "seq", "tp"),
        P(None, "tp"),
        P(None, None, None, "tp"),
        P(None, None, "tp"),
        P(None, "tp"),
        P(None, "tp", None),
        P(None, None, "tp"),
        P(None, "tp"),
        P(None, "tp"),
        P(None, "tp", None),
        P(None, "seq", "tp"),
        P(),
        P(),
    )
    return jax.shard_map(
        on_device,
        mesh=mesh,
        in_specs=placed,
        out_specs=(
            P(None, "seq", "tp"),
            P(None, "seq", "tp"),
            P(None, "tp"),
            P(None, "seq", None, "tp"),
            P(None, None, "tp"),
            P(None, "tp"),
            P(None, "tp", "seq"),
            P(None, "tp", None),
            P(None, "seq", "tp"),
            P(None, "tp"),
            P(None, "tp"),
            P(None, "tp", "seq"),
        ),
        check_vma=False,
    )
```

```python
import functools
import jax
import jax.numpy as jnp
import numpy as np
from jax import lax
from jax.experimental import pallas as pl
from jax.experimental.pallas import tpu as pltpu
from jax.sharding import PartitionSpec as P

CH = 16
LANES = 128
VMEM_BYTES = 20 * 1024 * 1024
BLOCK = 128
norm_epsilon = 1e-05
F32 = jnp.float32
LOW = jnp.bfloat16


def tables(states):
    wide = CH * states
    rows = np.arange(wide)
    lanes = np.arange(LANES)
    repeat = (rows[:, None] // states == np.arange(CH)[None, :]).astype(np.float32)
    picks = [lanes[:, None] == group * states + rows[None, :] % states for group in (0, 1, 3)]
    diagonal = (np.arange(CH)[:, None] == rows[None, :] // states).astype(np.float32)
    fold = (np.arange(3 * LANES)[:, None] // LANES == lanes[None, :] // states).astype(np.float32)
    fold_own = (rows[:, None] % states == lanes[None, :] % states).astype(np.float32)
    low = lambda value: jnp.asarray(value, LOW)
    return dict(
        pick=low(np.stack(picks).astype(np.float32)),
        diagonal=jnp.asarray(diagonal, F32),
        fold=low(fold),
        fold_own=jnp.asarray(fold_own, F32),
        gather=low(repeat.T),
    )


def dot(left, right):
    return jnp.dot(left, right, preferred_element_type=F32)


def spread_rows(table, row, states):
    wide = jnp.broadcast_to(table[:, row : row + 1], (table.shape[0], LANES))
    return [wide[at : at + states] for at in range(0, 4 * states, states)]


def groups(width):
    return [slice(at, at + LANES) for at in range(0, width, LANES)]


def row_of(ref, at, lanes):
    return ref[at : at + 1, lanes]


def summary_kernel(
    states, r_ref, act_ref, col_ref, out_ref, *scratch
):
    feed_refs = scratch[0:2]
    decay_ref, state_ref = scratch[2:]
    step = pl.program_id(1)
    r_ref, act_ref, col_ref = r_ref.at[0], act_ref.at[0], col_ref.at[0]
    count = r_ref.shape[0] // CH
    parts = groups(r_ref.shape[1])

    @pl.when(step == 0)
    def _():
        decay_ref[...] = jnp.ones_like(decay_ref)
        state_ref[...] = jnp.zeros_like(state_ref)

    def prepare(index, which):
        rows = pl.ds(pl.multiple_of(index * CH, CH), CH)
        feed_refs[which][...] = r_ref[rows, :] * act_ref[rows, :].astype(F32)

    def process(index, which, decays, values):
        base = pl.multiple_of(index * CH, CH)
        rates = r_ref.at[pl.ds(base, CH)]
        table, feeds = col_ref[pl.ds(base, CH), :].T[: 4 * states], feed_refs[which]
        for row in range(CH):
            mine = slice(row * states, (row + 1) * states)
            key, square, keep, _ = spread_rows(table, row, states)
            for at, lanes in enumerate(parts):
                decay = keep - row_of(rates, row, lanes) * square
                values[at] = decay * values[at] + row_of(feeds, row, lanes) * key
                decays[at] = decays[at] * decay

    prepare(0, 0)

    def pair(turn, carry):
        decays, values = list(carry[0]), list(carry[1])
        prepare(2 * turn + 1, 1)
        process(2 * turn, 0, decays, values)
        prepare(jnp.minimum(2 * turn + 2, count - 1), 0)
        process(2 * turn + 1, 1, decays, values)
        return (tuple(decays), tuple(values))

    start = (
        tuple(decay_ref[:, lanes] for lanes in parts),
        tuple(state_ref[:, lanes] for lanes in parts),
    )
    decays, values = lax.fori_loop(0, count // 2, pair, start)
    for at, lanes in enumerate(parts):
        decay_ref[:, lanes] = decays[at]
        state_ref[:, lanes] = values[at]

    @pl.when(step == pl.num_programs(1) - 1)
    def _():
        out_ref[0, :states] = decay_ref[...].astype(out_ref.dtype)
        out_ref[0, states:] = state_ref[...].astype(out_ref.dtype)


def forward_kernel(
    states,
    r_ref,
    act_ref,
    col_ref,
    gate_ref,
    skip_ref,
    in_ref,
    pick_ref,
    diagonal_ref,
    states_ref,
    mixed_ref,
    gated_ref,
    *scratch,
):
    feed_refs, value_refs, (state_ref,) = scratch[0:2], scratch[2:4], scratch[4:]
    step = pl.program_id(1)
    r_ref, act_ref, col_ref, gate_ref = r_ref.at[0], act_ref.at[0], col_ref.at[0], gate_ref.at[0]
    states_ref, mixed_ref, gated_ref = states_ref.at[0], mixed_ref.at[0], gated_ref.at[0]
    count = r_ref.shape[0] // CH
    parts = groups(r_ref.shape[1])

    @pl.when(step == 0)
    def _():
        state_ref[...] = in_ref[0].astype(F32)

    def prepare(index, which):
        rows = pl.ds(pl.multiple_of(index * CH, CH), CH)
        feed_refs[which][...] = r_ref[rows, :] * act_ref[rows, :].astype(F32)

    def process(index, which, values):
        base = pl.multiple_of(index * CH, CH)
        rates = r_ref.at[pl.ds(base, CH)]
        first = pl.multiple_of(index * (CH * states), CH * states)
        table, feeds = col_ref[pl.ds(base, CH), :].T[: 4 * states], feed_refs[which]
        for row in range(CH):
            mine = slice(row * states, (row + 1) * states)
            key, square, keep, _ = spread_rows(table, row, states)
            for at, lanes in enumerate(parts):
                decay = keep - row_of(rates, row, lanes) * square
                values[at] = decay * values[at] + row_of(feeds, row, lanes) * key
                low = values[at].astype(LOW)
                states_ref[pl.ds(first + row * states, states), lanes] = low
                value_refs[which][mine, lanes] = low

    def finish(index, which):
        rows = pl.ds(pl.multiple_of(index * CH, CH), CH)
        query = (dot(col_ref[rows, :].astype(LOW), pick_ref[2]) * diagonal_ref[...]).astype(LOW)
        recurrent = dot(query, value_refs[which][...])
        mixed = recurrent + skip_ref[...] * act_ref[rows, :].astype(F32)
        gate = gate_ref[rows, :].astype(F32)
        mixed_ref[rows, :] = mixed.astype(mixed_ref.dtype)
        gated_ref[rows, :] = (mixed * gate / (1.0 + jnp.exp(-gate))).astype(gated_ref.dtype)

    prepare(0, 0)

    def pair(turn, carry):
        values = list(carry)
        finish(jnp.maximum(2 * turn - 1, 0), 1)
        prepare(2 * turn + 1, 1)
        process(2 * turn, 0, values)
        finish(2 * turn, 0)
        prepare(jnp.minimum(2 * turn + 2, count - 1), 0)
        process(2 * turn + 1, 1, values)
        return tuple(values)

    values = lax.fori_loop(0, count // 2, pair, tuple(state_ref[:, lanes] for lanes in parts))
    finish(count - 1, 1)
    for at, lanes in enumerate(parts):
        state_ref[:, lanes] = values[at]


def adjoint_kernel(
    states, r_ref, gm_ref, col_ref, out_ref, *scratch
):
    (carry_ref,) = scratch
    step = pl.program_id(1)
    r_ref, gm_ref, col_ref = r_ref.at[0], gm_ref.at[0], col_ref.at[0]
    count = r_ref.shape[0] // CH
    parts = groups(r_ref.shape[1])

    @pl.when(step == 0)
    def _():
        carry_ref[...] = jnp.zeros_like(carry_ref)


    def process(index, which, values):
        base = pl.multiple_of(index * CH, CH)
        rates = r_ref.at[pl.ds(base, CH)]
        grads = gm_ref.at[pl.ds(base, CH)]
        table = col_ref[pl.ds(base, CH), :].T[: 4 * states]
        for row in reversed(range(CH)):
            mine = slice(row * states, (row + 1) * states)
            _, square, keep, query = spread_rows(table, row, states)
            for at, lanes in enumerate(parts):
                adjoint = query * row_of(grads, row, lanes) + values[at]
                values[at] = (keep - row_of(rates, row, lanes) * square) * adjoint


    def pair(turn, carry):
        values = list(carry)
        index = count - 1 - 2 * turn
        process(index, 0, values)
        process(index - 1, 1, values)
        return tuple(values)

    values = lax.fori_loop(0, count // 2, pair, tuple(carry_ref[:, lanes] for lanes in parts))
    for at, lanes in enumerate(parts):
        carry_ref[:, lanes] = values[at]

    @pl.when(step == pl.num_programs(1) - 1)
    def _():
        out_ref[0] = carry_ref[...].astype(out_ref.dtype)


def backward_kernel(
    states,
    r_ref,
    act_ref,
    gm_ref,
    col_ref,
    skip_ref,
    states_ref,
    before_ref,
    in_ref,
    carry_in_ref,
    pick_ref,
    diagonal_ref,
    fold_ref,
    fold_own_ref,
    gather_ref,
    rate_ref,
    gact_ref,
    sums_ref,
    *scratch,
):
    feed_refs, adjoint_refs, product_refs, part_refs = (
        scratch[2 * at : 2 * at + 2] for at in range(4)
    )
    first_ref, carry_ref = scratch[8:]
    step = pl.program_id(1)
    last = pl.num_programs(1) - 1
    r_ref, act_ref, gm_ref, col_ref = r_ref.at[0], act_ref.at[0], gm_ref.at[0], col_ref.at[0]
    states_ref, rate_ref, gact_ref, sums_ref = (
        states_ref.at[0],
        rate_ref.at[0],
        gact_ref.at[0],
        sums_ref.at[0],
    )
    count = r_ref.shape[0] // CH
    parts = groups(r_ref.shape[1])

    @pl.when(step == 0)
    def _():
        carry_ref[...] = carry_in_ref[0].astype(F32)

    @pl.when(step == last)
    def _():
        first_ref[...] = in_ref[0].astype(LOW)

    @pl.when(step != last)
    def _():
        first_ref[...] = before_ref[0]

    def prepare(index, which):
        rows = pl.ds(pl.multiple_of(index * CH, CH), CH)
        feed_refs[which][...] = r_ref[rows, :] * act_ref[rows, :].astype(F32)

    def process(index, which, values, held):
        base = pl.multiple_of(index * CH, CH)
        rates = r_ref.at[pl.ds(base, CH)]
        grads = gm_ref.at[pl.ds(base, CH)]
        first = pl.multiple_of(index * (CH * states), CH * states)
        table, feeds = col_ref[pl.ds(base, CH), :].T[: 4 * states], feed_refs[which]
        for row in reversed(range(CH)):
            mine = slice(row * states, (row + 1) * states)
            _, square, keep, query = spread_rows(table, row, states)
            sums = [None, None, None]
            for at, lanes in enumerate(parts):
                rate = row_of(rates, row, lanes)
                grad = row_of(grads, row, lanes)
                if row:
                    previous = states_ref[pl.ds(first + (row - 1) * states, states), lanes]
                else:
                    before = pl.multiple_of(jnp.maximum(first - states, 0), states)
                    previous = jnp.where(
                        index == 0, first_ref[:, lanes], states_ref[pl.ds(before, states), lanes]
                    )
                previous = previous.astype(F32)
                adjoint = query * grad + values[at]
                product = adjoint * previous
                values[at] = (keep - rate * square) * adjoint
                adjoint_refs[which][mine, lanes] = adjoint.astype(LOW)
                product_refs[which][mine, lanes] = product.astype(LOW)
                terms = (adjoint * row_of(feeds, row, lanes), product * rate, held[at] * grad)
                for kind, term in enumerate(terms):
                    sums[kind] = term if sums[kind] is None else sums[kind] + term
                held[at] = previous
            for kind in range(3):
                part_refs[which][mine, kind * LANES : (kind + 1) * LANES] = sums[kind].astype(LOW)

    def finish(index, which):
        rows = pl.ds(pl.multiple_of(index * CH, CH), CH)
        cols = col_ref[rows, :].astype(LOW)
        keys = (dot(cols, pick_ref[0]) * diagonal_ref[...]).astype(LOW)
        squares = (dot(cols, pick_ref[1]) * diagonal_ref[...]).astype(LOW)
        through_key = dot(keys, adjoint_refs[which][...])
        through_decay = dot(squares, product_refs[which][...])
        rate_ref[rows, :] = act_ref[rows, :].astype(F32) * through_key - through_decay
        gact_ref[rows, :] = r_ref[rows, :] * through_key + skip_ref[...] * gm_ref[rows, :]
        folded = dot(part_refs[which][...], fold_ref[...]) * fold_own_ref[...]
        high = folded.astype(LOW)
        rest = (folded - high.astype(F32)).astype(LOW)
        sums_ref[rows, :] = dot(gather_ref[...], high) + dot(gather_ref[...], rest)

    prepare(count - 1, 0)

    def pair(turn, carry):
        values, held = list(carry[0]), list(carry[1])
        index = count - 1 - 2 * turn
        finish(jnp.minimum(index + 1, count - 1), 1)
        prepare(index - 1, 1)
        process(index, 0, values, held)
        finish(index, 0)
        prepare(jnp.maximum(index - 2, 0), 0)
        process(index - 1, 1, values, held)
        return (tuple(values), tuple(held))

    tail = pl.ds((count * CH - 1) * states, states)
    start = (
        tuple(carry_ref[:, lanes] for lanes in parts),
        tuple(states_ref[tail, lanes].astype(F32) for lanes in parts),
    )
    values, _ = lax.fori_loop(0, count // 2, pair, start)
    finish(0, 1)
    for at, lanes in enumerate(parts):
        carry_ref[:, lanes] = values[at]


def plan(rate):
    batch, rows, channels = rate.shape
    block = BLOCK if rows % BLOCK == 0 else rows
    return batch, rows, channels, block, (batch, rows // block)


def cost(rate, states, work):
    size = rate.shape[0] * rate.shape[1] * rate.shape[2] * states
    return pl.CostEstimate(flops=size * work, bytes_accessed=size * 2, transcendentals=0)


def params(limit=VMEM_BYTES):
    return pltpu.CompilerParams(
        dimension_semantics=("arbitrary", "arbitrary"), vmem_limit_bytes=limit
    )


def whole(value):
    return pl.BlockSpec(value.shape, lambda m, b: (0,) * value.ndim)


def run_summary(rate, act, cols, states):
    batch, rows, channels, block, grid = plan(rate)
    part = pl.BlockSpec((1, block, channels), lambda m, b: (m, b, 0))
    narrow = pl.BlockSpec((1, block, LANES), lambda m, b: (m, b, 0))
    return pl.pallas_call(
        functools.partial(summary_kernel, states),
        grid=grid,
        in_specs=[part, part, narrow],
        out_specs=pl.BlockSpec((1, 2 * states, channels), lambda m, b: (m, 0, 0)),
        out_shape=jax.ShapeDtypeStruct((batch, 2 * states, channels), LOW),
        scratch_shapes=[pltpu.VMEM((CH, channels), F32)] * 2
        + [pltpu.VMEM((states, channels), F32)] * 2,
        compiler_params=params(),
        cost_estimate=cost(rate, states, 6),
    )(rate, act, cols)


def run_forward(rate, act, cols, gate, skip, incoming, states, table, limit):
    batch, rows, channels, block, grid = plan(rate)
    part = pl.BlockSpec((1, block, channels), lambda m, b: (m, b, 0))
    narrow = pl.BlockSpec((1, block, LANES), lambda m, b: (m, b, 0))
    edge = pl.BlockSpec((1, states, channels), lambda m, b: (m, 0, 0))
    consts = [table[name] for name in ("pick", "diagonal")]
    return pl.pallas_call(
        functools.partial(forward_kernel, states),
        grid=grid,
        in_specs=[part, part, narrow, part, whole(skip), edge] + [whole(value) for value in consts],
        out_specs=[
            pl.BlockSpec((1, block * states, channels), lambda m, b: (m, b, 0)),
            part,
            part,
        ],
        out_shape=[
            jax.ShapeDtypeStruct((batch, rows * states, channels), LOW),
            jax.ShapeDtypeStruct((batch, rows, channels), LOW),
            jax.ShapeDtypeStruct((batch, rows, channels), LOW),
        ],
        scratch_shapes=[pltpu.VMEM((CH, channels), F32)] * 2
        + [pltpu.VMEM((CH * states, channels), LOW)] * 2
        + [pltpu.VMEM((states, channels), F32)],
        compiler_params=params(limit),
        cost_estimate=cost(rate, states, 8),
    )(rate, act, cols, gate, skip, incoming, *consts)


def run_adjoint(rate, grad_mixed, cols, states):
    batch, rows, channels, block, grid = plan(rate)
    final = rows // block - 1
    part = pl.BlockSpec((1, block, channels), lambda m, b: (m, final - b, 0))
    narrow = pl.BlockSpec((1, block, LANES), lambda m, b: (m, final - b, 0))
    return pl.pallas_call(
        functools.partial(adjoint_kernel, states),
        grid=grid,
        in_specs=[part, part, narrow],
        out_specs=pl.BlockSpec((1, states, channels), lambda m, b: (m, 0, 0)),
        out_shape=jax.ShapeDtypeStruct((batch, states, channels), LOW),
        scratch_shapes=[pltpu.VMEM((states, channels), F32)],
        compiler_params=params(),
        cost_estimate=cost(rate, states, 5),
    )(rate, grad_mixed, cols)


def run_backward(
    rate, act, grad_mixed, cols, skip, kept_states, incoming, carry, states, table, limit
):
    batch, rows, channels, block, grid = plan(rate)
    final = rows // block - 1
    part = pl.BlockSpec((1, block, channels), lambda m, b: (m, final - b, 0))
    narrow = pl.BlockSpec((1, block, LANES), lambda m, b: (m, final - b, 0))
    edge = pl.BlockSpec((1, states, channels), lambda m, b: (m, 0, 0))
    names = ("pick", "diagonal", "fold", "fold_own", "gather")
    consts = [table[name] for name in names]
    return pl.pallas_call(
        functools.partial(backward_kernel, states),
        grid=grid,
        in_specs=[
            part,
            part,
            part,
            narrow,
            whole(skip),
            pl.BlockSpec((1, block * states, channels), lambda m, b: (m, final - b, 0)),
            pl.BlockSpec(
                (1, states, channels),
                lambda m, b: (m, jnp.maximum((final - b) * block - 1, 0), 0),
            ),
            edge,
            edge,
        ]
        + [whole(value) for value in consts],
        out_specs=[part, part, narrow],
        out_shape=[
            jax.ShapeDtypeStruct((batch, rows, channels), F32),
            jax.ShapeDtypeStruct((batch, rows, channels), F32),
            jax.ShapeDtypeStruct((batch, rows, LANES), F32),
        ],
        scratch_shapes=[pltpu.VMEM((CH, channels), F32)] * 2
        + [pltpu.VMEM((CH * states, channels), LOW)] * 4
        + [pltpu.VMEM((CH * states, 3 * LANES), LOW)] * 2
        + [pltpu.VMEM((states, channels), LOW), pltpu.VMEM((states, channels), F32)],
        compiler_params=params(limit),
        cost_estimate=cost(rate, states, 16),
    )(rate, act, grad_mixed, cols, skip, kept_states, kept_states, incoming, carry, *consts)


def columns(key, query, keep):
    kept = jnp.broadcast_to(keep[:, :, None], key.shape)
    parts = [key, kept * key * key, kept, query]
    blank = jnp.zeros(key.shape[:2] + (LANES - 4 * key.shape[2],), F32)
    return jnp.concatenate(parts + [blank], axis=2)


def shifted(value, axis, steps):
    count = lax.axis_size(axis)
    leading, last = (max(0, -steps), min(count, count - steps))
    return lax.ppermute(value, axis, [(source, source + steps) for source in range(leading, last)])


def swapped(value, axis, bit):
    count = lax.axis_size(axis)
    return lax.ppermute(value, axis, [(source, source ^ bit) for source in range(count)])


def odd(axis, bit):
    return (lax.axis_index(axis) // bit) % 2 == 1


def tp_bits():
    count = lax.axis_size("tp")
    return [1 << at for at in range(count.bit_length() - 1)]


def tp_sum(value, kind):
    for bit in tp_bits():
        value = value + swapped(value.astype(kind), "tp", bit).astype(F32)
    return value


def tp_gather(value, beside=None):
    pieces = {0: value}
    for bit in reversed(tp_bits()):
        for at in list(pieces):
            pieces[at + bit] = swapped(pieces[at], "tp", bit)
        if beside is not None and bit == tp_bits()[-1]:
            pieces[bit], beside = lax.optimization_barrier((pieces[bit], beside))
    ordered = [pieces[at] for at in range(len(pieces))]
    for bit in tp_bits():
        flip = odd("tp", bit)
        ordered = [
            jnp.where(flip, ordered[at ^ bit], ordered[at]) for at in range(len(ordered))
        ]
    gathered = jnp.concatenate(ordered, axis=-1)
    return gathered if beside is None else (gathered, beside)


def crossing(value):
    rows = value.shape[0] // 2
    return [swapped(value[:rows], "seq", 1), swapped(value[rows:], "seq", 1)]


def tp_scatter(value, beside=None):
    count = lax.axis_size("tp")
    width = value.shape[-1] // count
    parts = [value[..., at * width : (at + 1) * width] for at in range(count)]
    for bit in tp_bits():
        flip = odd("tp", bit)
        pairs = [(parts[2 * at], parts[2 * at + 1]) for at in range(len(parts) // 2)]
        sent = [jnp.where(flip, even, other).astype(LOW) for even, other in pairs]
        mine = [jnp.where(flip, other, even) for even, other in pairs]
        got = [swapped(there, "tp", bit) for there in sent]
        if beside is not None and bit == tp_bits()[-1]:
            got, beside = lax.optimization_barrier((got, beside))
        parts = [here + there.astype(F32) for here, there in zip(mine, got)]
    return parts[0] if beside is None else (parts[0], beside)


def scan_exclusive(decay, value, direction, beside=None):
    count = lax.axis_size("seq")
    states = decay.shape[1]
    outer = None
    step = 1
    while step < count:
        packed = jnp.concatenate([decay, value], axis=1).astype(LOW)
        final = 2 * step >= count
        got = shifted(packed[:, states:] if final else packed, "seq", direction * step)
        if beside is not None and step == 1:
            got, beside = lax.optimization_barrier((got, beside))
        got = got.astype(F32)
        if final:
            got_value = got
        else:
            got_decay, got_value = got[:, :states], got[:, states:]
        if outer is None:
            outer = (got_decay, got_value) if not final else (None, got_value)
        else:
            total, held = outer
            outer = (None if final else total * got_decay, total * got_value + held)
        if not final:
            value = decay * got_value + value
            decay = decay * got_decay
        step *= 2
    return outer[1] if beside is None else (outer[1], beside)


def after(value, *anchors):
    return lax.optimization_barrier((value,) + anchors)[0]


def other_half(value, anchor):
    count = lax.axis_size("seq") // lax.axis_size("tp")
    width = value.shape[-1] // count
    flip = odd("seq", 1)
    blocks = [value[..., at * width : (at + 1) * width] for at in range(count)]
    picked = [jnp.where(flip, blocks[at], blocks[at + 1]) for at in range(0, count, 2)]
    local = jnp.concatenate(picked, axis=-1).reshape(-1, value.shape[-1] // 2)
    return tp_gather(swapped(after(local, anchor), "seq", 1))


def store_products(out_ref, at, count, total):
    parts, block, width = out_ref.shape[0], out_ref.shape[1], out_ref.shape[2] // count
    for part in range(parts):
        rows = total[part * block : (part + 1) * block]
        out_ref[part, :, at * width : (at + 1) * width] = rows.astype(LOW)


def product(left, right):
    return lax.dot_general(left, right, (((0,), (0,)), ((), ())), preferred_element_type=F32)


def pair_kernel(count, side_ref, *refs):
    for at in range(count):
        left, left_other, right, right_other = (ref[...] for ref in refs[4 * at : 4 * at + 4])
        total = product(left, right) + product(left_other, right_other)
        store_products(refs[-1], at, count, total)


def plain_kernel(count, *refs):
    for at in range(count):
        total = product(refs[2 * at][...], refs[2 * at + 1][...])
        store_products(refs[-1], at, count, total)


def product_params(rows, width, total):
    return dict(
        compiler_params=pltpu.CompilerParams(
            dimension_semantics=("arbitrary",), vmem_limit_bytes=56 * 1024 * 1024
        ),
        cost_estimate=pl.CostEstimate(
            flops=2 * rows * width * total, bytes_accessed=4 * rows * total, transcendentals=0
        ),
    )


def own_half(value, other=0):
    count = lax.axis_size("seq")
    width = value.shape[-1] // count
    flip = odd("seq", 1)
    blocks = [value[..., at * width : (at + 1) * width] for at in range(count)]
    picked = [
        jnp.where(flip, blocks[at + 1 - other], blocks[at + other]) for at in range(0, count, 2)
    ]
    return jnp.concatenate(picked, axis=-1)


def pair_products(pieces):
    rows, width = pieces[0][0].shape
    channels = pieces[0][2].shape[1]
    parts = lax.axis_size("seq")
    block = width // parts
    group = max(1, LANES // block)
    side = (lax.axis_index("seq") % 2).astype(jnp.int32).reshape(1)
    specs, operands = [], []
    contiguous = pl.BlockSpec((rows, block * group), lambda at, side: (0, at))
    strided = pl.BlockSpec((rows, block), lambda at, side: (0, 2 * at + side[0]))
    full = pl.BlockSpec((rows, channels), lambda at, side: (0, 0))
    for left, left_other, right, right_other in pieces:
        specs += [strided if group == 1 else contiguous, contiguous, full, full]
        operands += [left if group == 1 else own_half(left), left_other, right, right_other]
    total = len(pieces) * channels
    return pl.pallas_call(
        functools.partial(pair_kernel, len(pieces)),
        grid_spec=pltpu.PrefetchScalarGridSpec(
            num_scalar_prefetch=1,
            grid=(parts // 2 // group,),
            in_specs=specs,
            out_specs=pl.BlockSpec((group, block, total), lambda at, side: (at, 0, 0)),
        ),
        out_shape=jax.ShapeDtypeStruct((parts // 2, block, total), LOW),
        **product_params(rows, width, total),
    )(side, *operands)


def plain_products(pieces):
    rows, width = pieces[0][0].shape
    channels = pieces[0][1].shape[1]
    parts = lax.axis_size("seq")
    block = width // parts
    group = max(1, LANES // block)
    total = len(pieces) * channels
    specs = [
        pl.BlockSpec((rows, block * group), lambda at: (0, at)),
        pl.BlockSpec((rows, channels), lambda at: (0, 0)),
    ] * len(pieces)
    return pl.pallas_call(
        functools.partial(plain_kernel, len(pieces)),
        grid=(parts // group,),
        in_specs=specs,
        out_specs=pl.BlockSpec((group, block, total), lambda at: (at, 0, 0)),
        out_shape=jax.ShapeDtypeStruct((parts, block, total), LOW),
        **product_params(rows, width, total),
    )(*[operand for piece in pieces for operand in piece])


def line_scatter(value):
    count = lax.axis_size("seq")
    groups = [list(range(side, count, 2)) for side in range(2)]
    return lax.psum_scatter(
        value, "seq", scatter_dimension=0, axis_index_groups=groups, tiled=True
    )[0]


def line_task(make):
    anchor = yield
    value = make(anchor)
    long = lax.axis_size("seq") // 2
    place = lax.axis_index("seq") // 2
    pairs = lambda sources, move: [
        (2 * source + side, 2 * (source + move) + side) for source in sources for side in range(2)
    ]
    pick = lambda at: lax.dynamic_index_in_dim(value, jnp.clip(at, 0, long - 1), 0, False)
    right, left = None, None
    for step in range(1, long):
        ahead = pick(place + long - step)
        behind = pick(place - long + step)
        if right is not None:
            right, left, anchor = lax.optimization_barrier((right, left, anchor))
            ahead = (ahead.astype(F32) + right.astype(F32)).astype(LOW)
            behind = (behind.astype(F32) + left.astype(F32)).astype(LOW)
        right = lax.ppermute(ahead, "seq", pairs(range(min(step, long - 1)), 1))
        left = lax.ppermute(behind, "seq", pairs(range(max(long - step, 1), long), -1))
        anchor = yield anchor
    own = pick(place).astype(F32)
    if right is not None:
        right, left, anchor = lax.optimization_barrier((right, left, anchor))
        own = own + right.astype(F32) + left.astype(F32)
    return own, anchor


def advance(tasks, results, anchor):
    if not tasks:
        return anchor
    name, task = tasks[0]
    try:
        return task.send(anchor)
    except StopIteration as ended:
        results[name], anchor = ended.value
        tasks.pop(0)
        return advance(tasks, results, anchor)


def add_task(tasks, name, make):
    task = line_task(make)
    next(task)
    tasks.append((name, task))


def small_task(scattered, summed):
    anchor = yield
    scattered, summed, anchor = lax.optimization_barrier((scattered, summed, anchor))
    bit = 1
    rows, channels = scattered.shape[1:]
    while bit < lax.axis_size("seq"):
        flip = odd("seq", bit)
        parted = scattered.reshape(-1, 2, rows, channels)
        low, high = parted[:, 0], parted[:, 1]
        sent = jnp.where(flip, low, high).astype(LOW).reshape(-1, channels)
        got = swapped(jnp.concatenate([sent, summed.astype(LOW)], axis=0), "seq", bit)
        anchor = yield anchor
        got, anchor = lax.optimization_barrier((got, anchor))
        scattered = jnp.where(flip, high, low).astype(F32)
        scattered = scattered + got[: sent.shape[0]].astype(F32).reshape(scattered.shape)
        summed = summed + got[sent.shape[0] :].astype(F32)
        bit *= 2
    return (scattered[0], summed), anchor


def gated_silu(argument):
    return argument * jax.nn.sigmoid(argument)


def silu_slope(argument):
    logistic = jax.nn.sigmoid(argument)
    return logistic * (1.0 + argument * (1.0 - logistic))


def doc_masks(doc_lengths, doc_offsets, positions):
    before = doc_offsets[:, None, :] <= positions[None, :, None]
    starts = jnp.max(jnp.where(before, doc_offsets[:, None, :], 0), axis=2)
    doc_ends = jnp.max(
        jnp.where(before, doc_offsets[:, None, :] + doc_lengths[:, None, :], 0), axis=2
    )
    return (starts, (positions[None, :] < doc_ends).astype(F32))


def matmul(left, right, dims):
    return jnp.einsum(dims, left, right, preferred_element_type=F32)


def conv_forward(conv_in, previous, conv_weight, conv_bias, tap_masks):
    edge = conv_weight.shape[0] - 1
    rows = conv_in.shape[1]
    extended = jnp.concatenate([previous, conv_in], axis=1).astype(F32)
    running = conv_bias.astype(F32)
    for back in range(edge + 1):
        window = extended[:, edge - back : edge - back + rows]
        running = running + conv_weight[back].astype(F32) * window * tap_masks[back][:, :, None]
    return (extended, running)


def rows_of(value):
    return value.reshape(-1, value.shape[-1])


def forward_layer(hidden, weights, valid_mask, keep_mask, tap_masks, table, side, inverse_gain, limit):
    gain, input_w, conv_weight, conv_bias, select_w, step_w, step_bias, skip, out_w = weights
    width = input_w.shape[0]
    scaled = (hidden * gain.astype(F32)).astype(LOW)
    complete, input_w = tp_gather(scaled, input_w)
    unscaled = complete.astype(F32) * inverse_gain
    square_sums = jnp.sum(unscaled * unscaled, axis=2)
    inverse_norm = lax.rsqrt(square_sums / width + norm_epsilon)
    normed_other = None if side is None else other_half(scaled, complete)
    projected = matmul(complete, input_w, "bph,htg->bptg")
    projected = (projected * inverse_norm[:, :, None, None]).astype(LOW)
    conv_in, gate_in = projected[:, :, 0, :], projected[:, :, 1, :]
    edge = conv_weight.shape[0] - 1
    rows = hidden.shape[1]
    previous = shifted(conv_in[:, rows - edge :], "seq", 1)
    extended, conv_out = conv_forward(conv_in, previous, conv_weight, conv_bias, tap_masks)
    conv_act = gated_silu(conv_out).astype(LOW)
    selection = tp_sum(matmul(conv_act, select_w, "mri,ic->mrc"), LOW)
    rank = step_w.shape[0]
    states = (selection.shape[2] - rank) // 2
    low_rank = selection[:, :, :rank].astype(LOW)
    key_state = selection[:, :, rank : rank + states]
    query_state = selection[:, :, rank + states :]
    biased = matmul(low_rank, step_w, "mrk,ki->mri") + step_bias
    step_size = jax.nn.softplus(biased)
    key_norm = jnp.sum(key_state * key_state, axis=2)
    rate = step_size / (1.0 + step_size * key_norm[:, :, None])
    cols = columns(key_state, query_state, keep_mask)
    side_rows = None if side is None else tp_gather(after(side, rate))
    summary = run_summary(rate, conv_act, cols, states).astype(F32)
    decay_total, local_state = summary[:, :states], summary[:, states:]
    incoming = scan_exclusive(decay_total, local_state, 1)
    if side is not None:
        incoming, normed_other = lax.optimization_barrier((incoming, normed_other))
    skip_row = skip.astype(F32)[None]
    kept_states, mixed, gated = run_forward(
        rate, conv_act, cols, gate_in, skip_row, incoming, states, table, limit
    )
    if side is not None:
        gated, side_rows = lax.optimization_barrier((gated, side_rows))
    branch = tp_scatter(matmul(gated, out_w, "mri,id->mrd").astype(LOW))
    new_hidden = hidden + valid_mask[:, :, None] * branch
    kept = dict(
        hidden=hidden,
        inverse_norm=inverse_norm,
        complete=complete,
        normed_other=normed_other,
        conv_in=conv_in,
        gate_in=gate_in,
        extended=extended,
        conv_out=conv_out,
        conv_act=conv_act,
        low_rank=low_rank,
        key_state=key_state,
        cols=cols,
        biased=biased,
        key_norm=key_norm,
        rate=rate,
        decay_total=decay_total,
        incoming=incoming,
        kept_states=kept_states,
        mixed=mixed,
        gated=gated,
    )
    return (new_hidden, kept, input_w, side_rows)


def backward_layer(
    at,
    grad_new,
    weights,
    kept,
    valid_mask,
    keep_mask,
    tap_masks,
    table,
    tasks,
    results,
    waiting,
    ready,
    beside,
):
    gain, input_w, conv_weight, conv_bias, select_w, step_w, step_bias, skip, out_w = weights
    hidden, inverse_norm, rate, cols = (
        kept[name] for name in ("hidden", "inverse_norm", "rate", "cols")
    )
    conv_act, key_state = kept["conv_act"], kept["key_state"]
    width = input_w.shape[0]
    states = key_state.shape[2]
    rank = step_w.shape[0]
    skip_row = skip.astype(F32)[None]
    first = waiting is not None
    if ready is None:
        branch_local = (grad_new * valid_mask[:, :, None]).astype(LOW)
        branch_rows, last = tp_gather(branch_local, waiting[3][1])
        waiting = waiting[:3] + (jnp.concatenate([waiting[3][0], last], axis=0),)
    else:
        branch_rows = ready
    grad_gated = matmul(branch_rows, out_w, "mrd,id->mri")
    gate_in = kept["gate_in"].astype(F32)
    grad_mixed = grad_gated * gated_silu(gate_in)
    inverse = inverse_norm[:, :, None]
    grad_gate = grad_gated * kept["mixed"].astype(F32) * silu_slope(gate_in) * inverse
    grad_gate = grad_gate.astype(LOW)
    act_float = conv_act.astype(F32)
    skip_grad = jnp.sum(grad_mixed * act_float, axis=(0, 1))
    normed = rows_of(kept["complete"])
    local_carry = run_adjoint(rate, grad_mixed, cols, states)
    carried = scan_exclusive(kept["decay_total"], local_carry.astype(F32), -1)
    if first:
        carried, results[("early", at + 1)] = lax.optimization_barrier(
            (carried, results[("early", at + 1)])
        )
        last = pair_products([waiting])
        carried, last = lax.optimization_barrier((carried, last))
        results[("conv", at + 1)] = line_scatter(last).astype(F32)
    partial = plain_products(
        [
            (normed, rows_of(grad_gate)),
            (rows_of(branch_rows), rows_of(kept["gated"])),
        ]
    )
    carried, partial = lax.optimization_barrier((carried, partial))
    results[("early", at)] = lax.psum_scatter(partial, "seq", scatter_dimension=0, tiled=True)[0]
    grad_rate, grad_act, sums = run_backward(
        rate,
        conv_act,
        grad_mixed,
        cols,
        skip_row,
        kept["kept_states"],
        kept["incoming"],
        carried,
        states,
        table,
        2 * VMEM_BYTES,
    )
    if not first:
        normed_other = swapped(own_half(normed, 1), "seq", 1)
        grad_rate, beside, normed_other = lax.optimization_barrier(
            (grad_rate, beside, normed_other)
        )
    denominator = 1.0 + jax.nn.softplus(kept["biased"]) * kept["key_norm"][:, :, None]
    grad_step = grad_rate / (denominator * denominator)
    grad_norm_key = -jnp.sum(grad_rate * rate * rate, axis=2)
    grad_pre = grad_step * jax.nn.sigmoid(kept["biased"])
    stepbias_grad = jnp.sum(grad_pre, axis=(0, 1))
    grad_pre_low = grad_pre.astype(LOW)
    step_grad = matmul(kept["low_rank"], grad_pre_low, "mrk,mri->ki")
    grad_rank = matmul(grad_pre_low, step_w, "mri,ki->mrk")
    through_feed, through_decay, grad_query = (
        sums[:, :, at * states : (at + 1) * states] for at in range(3)
    )
    grad_key = (
        through_feed
        - 2.0 * keep_mask[:, :, None] * key_state * through_decay
        + 2.0 * key_state * grad_norm_key[:, :, None]
    )
    grad_selection = tp_sum(jnp.concatenate([grad_rank, grad_key, grad_query], axis=2), LOW)
    grad_selection = grad_selection.astype(LOW)
    select_full = matmul(grad_selection, conv_act, "mrc,mri->ci")
    grad_act = grad_act + matmul(grad_selection, select_w, "mrc,ic->mri")
    grad_conv = grad_act * silu_slope(kept["conv_out"])
    convbias_grad = jnp.sum(grad_conv, axis=(0, 1))
    edge = conv_weight.shape[0] - 1
    rows = grad_conv.shape[1]
    extended = kept["extended"]
    tap_grads = []
    grad_extended = jnp.zeros(extended.shape, F32)
    for back in range(edge + 1):
        masked = grad_conv * tap_masks[back][:, :, None]
        tap_grads.append(jnp.sum(masked * extended[:, edge - back : edge - back + rows], axis=(0, 1)))
        grad_extended = grad_extended + jnp.pad(
            masked * conv_weight[back].astype(F32), ((0, 0), (edge - back, back), (0, 0))
        )
    returned = shifted(grad_extended[:, :edge], "seq", -1)
    grad_conv_in = grad_extended[:, edge:] + jnp.pad(
        returned, ((0, 0), (rows - edge, 0), (0, 0))
    )
    grad_conv_in = (grad_conv_in * inverse).astype(LOW)
    conv_other = crossing(rows_of(grad_conv_in))
    if first:
        normed_other = kept["normed_other"]
    grad_projected = jnp.stack([grad_conv_in, grad_gate], axis=2)
    grad_normed = matmul(grad_projected, input_w, "bptg,htg->bph").astype(LOW)
    if first:
        grad_normed = tp_scatter(grad_normed)
        conv_other = jnp.concatenate(conv_other, axis=0)
    else:
        grad_normed, conv_first = tp_scatter(grad_normed, conv_other[0])
        conv_other = (conv_first, conv_other[1])
    grad_normed = grad_normed.astype(F32)
    conv_piece = (normed, normed_other, rows_of(grad_conv_in), conv_other)
    inner = tp_sum(
        jnp.sum(
            grad_conv_in.astype(F32) * kept["conv_in"].astype(F32)
            + grad_gate.astype(F32) * gate_in,
            axis=2,
        ),
        F32,
    )
    gain_grad = jnp.sum(grad_normed * hidden, axis=(0, 1))
    grad_hidden = (
        grad_new
        + gain.astype(F32) * grad_normed
        - hidden * (inverse_norm * inner / width)[:, :, None]
    )
    count = lax.axis_size("seq")
    scattered = jnp.stack([select_full[:rank], step_grad], axis=0)
    scattered = scattered.reshape(2, count, rank // count, -1).swapaxes(0, 1)
    channels = conv_act.shape[2]
    summed = jnp.concatenate(
        [
            jnp.stack(tap_grads + [convbias_grad, stepbias_grad, skip_grad], axis=0),
            select_full[rank:],
            jnp.pad(gain_grad, (0, channels - gain_grad.shape[0]))[None],
        ],
        axis=0,
    )
    return (grad_hidden, conv_piece, scattered, summed)


def on_device(
    tokens,
    norm_gain,
    input_weight,
    conv_weight,
    conv_bias,
    select_weight,
    step_weight,
    step_bias,
    skip_gain,
    out_weight,
    cotangent,
    doc_lengths,
    doc_offsets,
):
    rows = tokens.shape[1]
    positions = lax.axis_index("seq") * rows + jnp.arange(rows, dtype=jnp.int32)
    starts, valid_mask = doc_masks(doc_lengths, doc_offsets, positions)
    keep_mask = (positions[None, :] != starts).astype(F32)
    tap_masks = [
        (positions[None, :] - back >= starts).astype(F32) for back in range(conv_weight.shape[1])
    ]
    layers = input_weight.shape[0]
    table = tables((select_weight.shape[2] - step_weight.shape[1]) // 2)
    small = (conv_weight, conv_bias, select_weight, step_weight, step_bias, skip_gain, out_weight)
    shared = [tuple(member[at] for member in small) for at in range(layers)]
    hidden = tokens.astype(F32)
    grad = cotangent.astype(F32)
    side = (grad * valid_mask[:, :, None]).astype(LOW)
    inverse_gains = 1.0 / tp_gather(norm_gain.astype(F32))
    saved, inputs, ready = [], [None] * layers, None
    for at in range(layers):
        own = after(input_weight[at], hidden)
        hidden, kept, inputs[at], extra = forward_layer(
            hidden,
            (norm_gain[at], own) + shared[at],
            valid_mask,
            keep_mask,
            tap_masks,
            table,
            side if at == 0 else None,
            inverse_gains[at],
            2 * VMEM_BYTES,
        )
        ready = extra if at == 0 else ready
        saved.append(kept)
    layer_out = hidden.astype(LOW)
    tasks, results, waiting = [], {}, None
    scattered, summed = [None] * layers, [None] * layers
    for at in reversed(range(layers)):
        grad, waiting, scattered[at], summed[at] = backward_layer(
            at,
            grad,
            (norm_gain[at], inputs[at]) + shared[at],
            saved[at],
            valid_mask,
            keep_mask,
            tap_masks,
            table,
            tasks,
            results,
            waiting,
            ready if waiting is None else None,
            hidden if waiting is None else None,
        )
    piece = waiting
    add_task(tasks, ("conv", 0), lambda anchor: pair_products([piece]))
    rank = step_weight.shape[1]
    count = lax.axis_size("seq")
    packed = jnp.stack(scattered, axis=1).reshape(count, -1, out_weight.shape[1])
    small = small_task(packed, jnp.concatenate(summed, axis=0))
    next(small)
    extra = [("small", small)]
    while tasks or extra:
        grad = advance(tasks, results, grad)
        grad = advance(extra, results, grad)
    scattered, summed = results["small"]
    scattered = scattered.reshape(layers, 2, rank // count, -1)
    summed = summed.reshape(layers, -1, summed.shape[1])
    channels = out_weight.shape[1]
    parts = [
        [results[("early", at)][:, piece * channels : (piece + 1) * channels] for piece in range(2)]
        for at in range(layers)
    ]
    conv_parts = [results[("conv", at)] for at in range(layers)]
    gate_parts = [parts[at][0].astype(F32) for at in range(layers)]
    out_parts = [parts[at][1].astype(F32) for at in range(layers)]
    edge = conv_weight.shape[1]
    blank = [jnp.zeros_like(conv_parts[0])] + conv_parts[1:]
    inweight_grad = jnp.stack(
        [jnp.stack([conv, gate], axis=1) for conv, gate in zip(blank, gate_parts)], axis=0
    )
    inweight_grad = lax.dynamic_update_slice(
        after(inweight_grad, grad), conv_parts[0][None, :, None, :], (0, 0, 0, 0)
    )
    return (
        layer_out,
        grad.astype(LOW),
        summed[:, -1, : norm_gain.shape[1]],
        inweight_grad,
        summed[:, :edge],
        summed[:, edge],
        jnp.swapaxes(scattered[:, 0], 1, 2),
        jnp.swapaxes(summed[:, edge + 3 : -1], 1, 2),
        scattered[:, 1],
        summed[:, edge + 1],
        summed[:, edge + 2],
        jnp.swapaxes(jnp.stack(out_parts, axis=0), 1, 2),
    )


def solution(mesh):
    placed = (
        P(None, "seq", "tp"),
        P(None, "tp"),
        P(None, None, None, "tp"),
        P(None, None, "tp"),
        P(None, "tp"),
        P(None, "tp", None),
        P(None, None, "tp"),
        P(None, "tp"),
        P(None, "tp"),
        P(None, "tp", None),
        P(None, "seq", "tp"),
        P(),
        P(),
    )
    return jax.shard_map(
        on_device,
        mesh=mesh,
        in_specs=placed,
        out_specs=(
            P(None, "seq", "tp"),
            P(None, "seq", "tp"),
            P(None, "tp"),
            P(None, "seq", None, "tp"),
            P(None, None, "tp"),
            P(None, "tp"),
            P(None, "tp", "seq"),
            P(None, "tp", None),
            P(None, "seq", "tp"),
            P(None, "tp"),
            P(None, "tp"),
            P(None, "tp", "seq"),
        ),
        check_vma=False,
    )
```

```python
import functools
import jax
import jax.numpy as jnp
import numpy as np
from jax import lax
from jax.experimental import pallas as pl
from jax.experimental.pallas import tpu as pltpu
from jax.sharding import PartitionSpec as P

CH = 16
LANES = 128
VMEM_BYTES = 20 * 1024 * 1024
BLOCK = 128
norm_epsilon = 1e-05
F32 = jnp.float32
LOW = jnp.bfloat16


def positions_of(shape, dimension):
    return lax.broadcasted_iota(jnp.int32, shape, dimension)


def fill_tables(states, pick_ref, diagonal_ref, fold_ref=None, own_ref=None):
    low, bits = states - 1, states.bit_length() - 1
    rows, lanes = positions_of(pick_ref.shape, 0), positions_of(pick_ref.shape, 1)
    pick_ref[...] = jnp.where(rows == (lanes & low), 1.0, 0.0).astype(LOW)
    diagonal_ref[...] = jnp.where(rows == (lanes >> bits), 1.0, 0.0).astype(F32)
    if fold_ref is not None:
        rows, lanes = positions_of(fold_ref.shape, 0), positions_of(fold_ref.shape, 1)
        same = (rows >> (LANES.bit_length() - 1)) == (lanes >> bits)
        fold_ref[...] = jnp.where(same, 1.0, 0.0).astype(LOW)
        rows, lanes = positions_of(own_ref.shape, 0), positions_of(own_ref.shape, 1)
        own_ref[...] = jnp.where((rows & low) == (lanes & low), 1.0, 0.0).astype(F32)


def dot(left, right):
    return jnp.dot(left, right, preferred_element_type=F32)


def spread_table(sel_ref, keep_ref, rows, states):
    start = sel_ref.shape[1] - 2 * states
    turned = sel_ref[rows, start:].T
    key, query = turned[:states], turned[states:]
    keep = keep_ref[rows, :].T[:states]
    return jnp.concatenate([key, keep * key * key, keep, query], axis=0)


def spread_rows(table, row, states):
    wide = jnp.broadcast_to(table[:, row : row + 1], (table.shape[0], LANES))
    return [wide[at : at + states] for at in range(0, 4 * states, states)]


def expanded(value, pick_ref, diagonal_ref):
    return (dot(value.astype(LOW), pick_ref[...]) * diagonal_ref[...]).astype(LOW)


def groups(width):
    return [slice(at, at + LANES) for at in range(0, width, LANES)]


def row_of(ref, at, lanes):
    return ref[at : at + 1, lanes]


def summary_kernel(
    states, r_ref, act_ref, sel_ref, keep_ref, out_ref, *scratch
):
    feed_refs = scratch[0:2]
    decay_ref, state_ref = scratch[2:]
    step = pl.program_id(1)
    r_ref, act_ref, sel_ref, keep_ref = r_ref.at[0], act_ref.at[0], sel_ref.at[0], keep_ref.at[0]
    count = r_ref.shape[0] // CH
    parts = groups(r_ref.shape[1])

    @pl.when(step == 0)
    def _():
        decay_ref[...] = jnp.ones_like(decay_ref)
        state_ref[...] = jnp.zeros_like(state_ref)

    def prepare(index, which):
        rows = pl.ds(pl.multiple_of(index * CH, CH), CH)
        feed_refs[which][...] = r_ref[rows, :] * act_ref[rows, :].astype(F32)

    def process(index, which, decays, values):
        base = pl.multiple_of(index * CH, CH)
        rates = r_ref.at[pl.ds(base, CH)]
        table, feeds = spread_table(sel_ref, keep_ref, pl.ds(base, CH), states), feed_refs[which]
        for row in range(CH):
            mine = slice(row * states, (row + 1) * states)
            key, square, keep, _ = spread_rows(table, row, states)
            for at, lanes in enumerate(parts):
                decay = keep - row_of(rates, row, lanes) * square
                values[at] = decay * values[at] + row_of(feeds, row, lanes) * key
                decays[at] = decays[at] * decay

    prepare(0, 0)

    def pair(turn, carry):
        decays, values = list(carry[0]), list(carry[1])
        prepare(2 * turn + 1, 1)
        process(2 * turn, 0, decays, values)
        prepare(jnp.minimum(2 * turn + 2, count - 1), 0)
        process(2 * turn + 1, 1, decays, values)
        return (tuple(decays), tuple(values))

    start = (
        tuple(decay_ref[:, lanes] for lanes in parts),
        tuple(state_ref[:, lanes] for lanes in parts),
    )
    decays, values = lax.fori_loop(0, count // 2, pair, start)
    for at, lanes in enumerate(parts):
        decay_ref[:, lanes] = decays[at]
        state_ref[:, lanes] = values[at]

    @pl.when(step == pl.num_programs(1) - 1)
    def _():
        out_ref[0, :states] = decay_ref[...].astype(out_ref.dtype)
        out_ref[0, states:] = state_ref[...].astype(out_ref.dtype)


def forward_kernel(
    states,
    r_ref,
    act_ref,
    sel_ref,
    keep_ref,
    gate_ref,
    skip_ref,
    in_ref,
    states_ref,
    mixed_ref,
    gated_ref,
    *scratch,
):
    feed_refs, value_refs = scratch[0:2], scratch[2:4]
    state_ref, pick_ref, diagonal_ref = scratch[4:]
    fill_tables(states, pick_ref, diagonal_ref)
    step = pl.program_id(1)
    r_ref, act_ref, sel_ref, gate_ref = r_ref.at[0], act_ref.at[0], sel_ref.at[0], gate_ref.at[0]
    keep_ref = keep_ref.at[0]
    states_ref, mixed_ref, gated_ref = states_ref.at[0], mixed_ref.at[0], gated_ref.at[0]
    count = r_ref.shape[0] // CH
    parts = groups(r_ref.shape[1])

    @pl.when(step == 0)
    def _():
        state_ref[...] = in_ref[0].astype(F32)

    def prepare(index, which):
        rows = pl.ds(pl.multiple_of(index * CH, CH), CH)
        feed_refs[which][...] = r_ref[rows, :] * act_ref[rows, :].astype(F32)

    def process(index, which, values):
        base = pl.multiple_of(index * CH, CH)
        rates = r_ref.at[pl.ds(base, CH)]
        first = pl.multiple_of(index * (CH * states), CH * states)
        table, feeds = spread_table(sel_ref, keep_ref, pl.ds(base, CH), states), feed_refs[which]
        for row in range(CH):
            mine = slice(row * states, (row + 1) * states)
            key, square, keep, _ = spread_rows(table, row, states)
            for at, lanes in enumerate(parts):
                decay = keep - row_of(rates, row, lanes) * square
                values[at] = decay * values[at] + row_of(feeds, row, lanes) * key
                low = values[at].astype(LOW)
                states_ref[pl.ds(first + row * states, states), lanes] = low
                value_refs[which][mine, lanes] = low

    def finish(index, which):
        rows = pl.ds(pl.multiple_of(index * CH, CH), CH)
        query = expanded(sel_ref[rows, sel_ref.shape[1] - states :], pick_ref, diagonal_ref)
        recurrent = dot(query, value_refs[which][...])
        mixed = recurrent + skip_ref[...] * act_ref[rows, :].astype(F32)
        gate = gate_ref[rows, :].astype(F32)
        mixed_ref[rows, :] = mixed.astype(mixed_ref.dtype)
        gated_ref[rows, :] = (mixed * gate / (1.0 + jnp.exp(-gate))).astype(gated_ref.dtype)

    prepare(0, 0)

    def pair(turn, carry):
        values = list(carry)
        finish(jnp.maximum(2 * turn - 1, 0), 1)
        prepare(2 * turn + 1, 1)
        process(2 * turn, 0, values)
        finish(2 * turn, 0)
        prepare(jnp.minimum(2 * turn + 2, count - 1), 0)
        process(2 * turn + 1, 1, values)
        return tuple(values)

    values = lax.fori_loop(0, count // 2, pair, tuple(state_ref[:, lanes] for lanes in parts))
    finish(count - 1, 1)
    for at, lanes in enumerate(parts):
        state_ref[:, lanes] = values[at]


def adjoint_kernel(
    states, r_ref, gm_ref, sel_ref, keep_ref, out_ref, *scratch
):
    (carry_ref,) = scratch
    step = pl.program_id(1)
    r_ref, gm_ref, sel_ref, keep_ref = r_ref.at[0], gm_ref.at[0], sel_ref.at[0], keep_ref.at[0]
    count = r_ref.shape[0] // CH
    parts = groups(r_ref.shape[1])

    @pl.when(step == 0)
    def _():
        carry_ref[...] = jnp.zeros_like(carry_ref)


    def process(index, which, values):
        base = pl.multiple_of(index * CH, CH)
        rates = r_ref.at[pl.ds(base, CH)]
        grads = gm_ref.at[pl.ds(base, CH)]
        table = spread_table(sel_ref, keep_ref, pl.ds(base, CH), states)
        for row in reversed(range(CH)):
            mine = slice(row * states, (row + 1) * states)
            _, square, keep, query = spread_rows(table, row, states)
            for at, lanes in enumerate(parts):
                adjoint = query * row_of(grads, row, lanes) + values[at]
                values[at] = (keep - row_of(rates, row, lanes) * square) * adjoint


    def pair(turn, carry):
        values = list(carry)
        index = count - 1 - 2 * turn
        process(index, 0, values)
        process(index - 1, 1, values)
        return tuple(values)

    values = lax.fori_loop(0, count // 2, pair, tuple(carry_ref[:, lanes] for lanes in parts))
    for at, lanes in enumerate(parts):
        carry_ref[:, lanes] = values[at]

    @pl.when(step == pl.num_programs(1) - 1)
    def _():
        out_ref[0] = carry_ref[...].astype(out_ref.dtype)


def backward_kernel(
    states,
    r_ref,
    act_ref,
    gm_ref,
    sel_ref,
    keep_ref,
    skip_ref,
    states_ref,
    before_ref,
    in_ref,
    carry_in_ref,
    rate_ref,
    gact_ref,
    sums_ref,
    *scratch,
):
    feed_refs, adjoint_refs, product_refs, part_refs = (
        scratch[2 * at : 2 * at + 2] for at in range(4)
    )
    first_ref, carry_ref, pick_ref, diagonal_ref, fold_ref, fold_own_ref = scratch[8:]
    fill_tables(states, pick_ref, diagonal_ref, fold_ref, fold_own_ref)
    step = pl.program_id(1)
    last = pl.num_programs(1) - 1
    r_ref, act_ref, gm_ref, sel_ref = r_ref.at[0], act_ref.at[0], gm_ref.at[0], sel_ref.at[0]
    keep_ref = keep_ref.at[0]
    states_ref, rate_ref, gact_ref, sums_ref = (
        states_ref.at[0],
        rate_ref.at[0],
        gact_ref.at[0],
        sums_ref.at[0],
    )
    count = r_ref.shape[0] // CH
    parts = groups(r_ref.shape[1])

    @pl.when(step == 0)
    def _():
        carry_ref[...] = carry_in_ref[0].astype(F32)

    @pl.when(step == last)
    def _():
        first_ref[...] = in_ref[0].astype(LOW)

    @pl.when(step != last)
    def _():
        first_ref[...] = before_ref[0]

    def prepare(index, which):
        rows = pl.ds(pl.multiple_of(index * CH, CH), CH)
        feed_refs[which][...] = r_ref[rows, :] * act_ref[rows, :].astype(F32)

    def process(index, which, values, held):
        base = pl.multiple_of(index * CH, CH)
        rates = r_ref.at[pl.ds(base, CH)]
        grads = gm_ref.at[pl.ds(base, CH)]
        first = pl.multiple_of(index * (CH * states), CH * states)
        table, feeds = spread_table(sel_ref, keep_ref, pl.ds(base, CH), states), feed_refs[which]
        for row in reversed(range(CH)):
            mine = slice(row * states, (row + 1) * states)
            _, square, keep, query = spread_rows(table, row, states)
            sums = [None, None, None]
            for at, lanes in enumerate(parts):
                rate = row_of(rates, row, lanes)
                grad = row_of(grads, row, lanes)
                if row:
                    previous = states_ref[pl.ds(first + (row - 1) * states, states), lanes]
                else:
                    before = pl.multiple_of(jnp.maximum(first - states, 0), states)
                    previous = jnp.where(
                        index == 0, first_ref[:, lanes], states_ref[pl.ds(before, states), lanes]
                    )
                previous = previous.astype(F32)
                adjoint = query * grad + values[at]
                product = adjoint * previous
                values[at] = (keep - rate * square) * adjoint
                adjoint_refs[which][mine, lanes] = adjoint.astype(LOW)
                product_refs[which][mine, lanes] = product.astype(LOW)
                terms = (adjoint * row_of(feeds, row, lanes), product * rate, held[at] * grad)
                for kind, term in enumerate(terms):
                    sums[kind] = term if sums[kind] is None else sums[kind] + term
                held[at] = previous
            for kind in range(3):
                part_refs[which][mine, kind * LANES : (kind + 1) * LANES] = sums[kind].astype(LOW)

    def finish(index, which):
        rows = pl.ds(pl.multiple_of(index * CH, CH), CH)
        start = sel_ref.shape[1] - 2 * states
        key = sel_ref[rows, start : start + states]
        kept_key = keep_ref[rows, :states] * key
        keys = expanded(key, pick_ref, diagonal_ref)
        squares = expanded(kept_key * key, pick_ref, diagonal_ref)
        through_key = dot(keys, adjoint_refs[which][...])
        through_decay = dot(squares, product_refs[which][...])
        rate_ref[rows, :] = act_ref[rows, :].astype(F32) * through_key - through_decay
        gact_ref[rows, :] = r_ref[rows, :] * through_key + skip_ref[...] * gm_ref[rows, :]
        folded = dot(part_refs[which][...], fold_ref[...]) * fold_own_ref[...]
        high = folded.astype(LOW)
        rest = (folded - high.astype(F32)).astype(LOW)
        gather = diagonal_ref[...].astype(LOW)
        total = dot(gather, high) + dot(gather, rest)
        grad_key = total[:, :states] - 2.0 * kept_key * total[:, states : 2 * states]
        sums_ref[rows, :start] = jnp.zeros((CH, start), F32)
        sums_ref[rows, start : start + states] = grad_key
        sums_ref[rows, start + states :] = total[:, 2 * states : 3 * states]

    prepare(count - 1, 0)

    def pair(turn, carry):
        values, held = list(carry[0]), list(carry[1])
        index = count - 1 - 2 * turn
        finish(jnp.minimum(index + 1, count - 1), 1)
        prepare(index - 1, 1)
        process(index, 0, values, held)
        finish(index, 0)
        prepare(jnp.maximum(index - 2, 0), 0)
        process(index - 1, 1, values, held)
        return (tuple(values), tuple(held))

    tail = pl.ds((count * CH - 1) * states, states)
    start = (
        tuple(carry_ref[:, lanes] for lanes in parts),
        tuple(states_ref[tail, lanes].astype(F32) for lanes in parts),
    )
    values, _ = lax.fori_loop(0, count // 2, pair, start)
    finish(0, 1)
    for at, lanes in enumerate(parts):
        carry_ref[:, lanes] = values[at]


def plan(rate):
    batch, rows, channels = rate.shape
    block = BLOCK if rows % BLOCK == 0 else rows
    return batch, rows, channels, block, (batch, rows // block)


def cost(rate, states, work):
    size = rate.shape[0] * rate.shape[1] * rate.shape[2] * states
    return pl.CostEstimate(flops=size * work, bytes_accessed=size * 2, transcendentals=0)


def params(limit=VMEM_BYTES):
    return pltpu.CompilerParams(
        dimension_semantics=("arbitrary", "arbitrary"), vmem_limit_bytes=limit
    )


def whole(value):
    return pl.BlockSpec(value.shape, lambda m, b: (0,) * value.ndim)


def table_shapes(states):
    return [
        pltpu.VMEM((states, CH * states), LOW),
        pltpu.VMEM((CH, CH * states), F32),
        pltpu.VMEM((3 * LANES, LANES), LOW),
        pltpu.VMEM((CH * states, LANES), F32),
    ]


def run_summary(rate, act, sel, keep, states):
    batch, rows, channels, block, grid = plan(rate)
    part = pl.BlockSpec((1, block, channels), lambda m, b: (m, b, 0))
    narrow = pl.BlockSpec((1, block, sel.shape[2]), lambda m, b: (m, b, 0))
    marks = pl.BlockSpec((1, block, LANES), lambda m, b: (m, b, 0))
    return pl.pallas_call(
        functools.partial(summary_kernel, states),
        grid=grid,
        in_specs=[part, part, narrow, marks],
        out_specs=pl.BlockSpec((1, 2 * states, channels), lambda m, b: (m, 0, 0)),
        out_shape=jax.ShapeDtypeStruct((batch, 2 * states, channels), LOW),
        scratch_shapes=[pltpu.VMEM((CH, channels), F32)] * 2
        + [pltpu.VMEM((states, channels), F32)] * 2,
        compiler_params=params(),
        cost_estimate=cost(rate, states, 6),
    )(rate, act, sel, keep)


def run_forward(rate, act, sel, keep, gate, skip, incoming, states, limit):
    batch, rows, channels, block, grid = plan(rate)
    part = pl.BlockSpec((1, block, channels), lambda m, b: (m, b, 0))
    narrow = pl.BlockSpec((1, block, sel.shape[2]), lambda m, b: (m, b, 0))
    marks = pl.BlockSpec((1, block, LANES), lambda m, b: (m, b, 0))
    edge = pl.BlockSpec((1, states, channels), lambda m, b: (m, 0, 0))
    return pl.pallas_call(
        functools.partial(forward_kernel, states),
        grid=grid,
        in_specs=[part, part, narrow, marks, part, whole(skip), edge],
        out_specs=[
            pl.BlockSpec((1, block * states, channels), lambda m, b: (m, b, 0)),
            part,
            part,
        ],
        out_shape=[
            jax.ShapeDtypeStruct((batch, rows * states, channels), LOW),
            jax.ShapeDtypeStruct((batch, rows, channels), LOW),
            jax.ShapeDtypeStruct((batch, rows, channels), LOW),
        ],
        scratch_shapes=[pltpu.VMEM((CH, channels), F32)] * 2
        + [pltpu.VMEM((CH * states, channels), LOW)] * 2
        + [pltpu.VMEM((states, channels), F32)]
        + table_shapes(states)[:2],
        compiler_params=params(limit),
        cost_estimate=cost(rate, states, 8),
    )(rate, act, sel, keep, gate, skip, incoming)


def run_adjoint(rate, grad_mixed, sel, keep, states):
    batch, rows, channels, block, grid = plan(rate)
    final = rows // block - 1
    part = pl.BlockSpec((1, block, channels), lambda m, b: (m, final - b, 0))
    narrow = pl.BlockSpec((1, block, sel.shape[2]), lambda m, b: (m, final - b, 0))
    marks = pl.BlockSpec((1, block, LANES), lambda m, b: (m, final - b, 0))
    return pl.pallas_call(
        functools.partial(adjoint_kernel, states),
        grid=grid,
        in_specs=[part, part, narrow, marks],
        out_specs=pl.BlockSpec((1, states, channels), lambda m, b: (m, 0, 0)),
        out_shape=jax.ShapeDtypeStruct((batch, states, channels), LOW),
        scratch_shapes=[pltpu.VMEM((states, channels), F32)],
        compiler_params=params(),
        cost_estimate=cost(rate, states, 5),
    )(rate, grad_mixed, sel, keep)


def run_backward(
    rate, act, grad_mixed, sel, keep, skip, kept_states, incoming, carry, states, limit
):
    batch, rows, channels, block, grid = plan(rate)
    final = rows // block - 1
    part = pl.BlockSpec((1, block, channels), lambda m, b: (m, final - b, 0))
    narrow = pl.BlockSpec((1, block, sel.shape[2]), lambda m, b: (m, final - b, 0))
    marks = pl.BlockSpec((1, block, LANES), lambda m, b: (m, final - b, 0))
    edge = pl.BlockSpec((1, states, channels), lambda m, b: (m, 0, 0))
    return pl.pallas_call(
        functools.partial(backward_kernel, states),
        grid=grid,
        in_specs=[
            part,
            part,
            part,
            narrow,
            marks,
            whole(skip),
            pl.BlockSpec((1, block * states, channels), lambda m, b: (m, final - b, 0)),
            pl.BlockSpec(
                (1, states, channels),
                lambda m, b: (m, jnp.maximum((final - b) * block - 1, 0), 0),
            ),
            edge,
            edge,
        ]
       ,
        out_specs=[part, part, narrow],
        out_shape=[
            jax.ShapeDtypeStruct((batch, rows, channels), F32),
            jax.ShapeDtypeStruct((batch, rows, channels), F32),
            jax.ShapeDtypeStruct((batch, rows, sel.shape[2]), F32),
        ],
        scratch_shapes=[pltpu.VMEM((CH, channels), F32)] * 2
        + [pltpu.VMEM((CH * states, channels), LOW)] * 4
        + [pltpu.VMEM((CH * states, 3 * LANES), LOW)] * 2
        + [pltpu.VMEM((states, channels), LOW), pltpu.VMEM((states, channels), F32)]
        + table_shapes(states),
        compiler_params=params(limit),
        cost_estimate=cost(rate, states, 16),
    )(rate, act, grad_mixed, sel, keep, skip, kept_states, kept_states, incoming, carry)


def shifted(value, axis, steps):
    count = lax.axis_size(axis)
    leading, last = (max(0, -steps), min(count, count - steps))
    return lax.ppermute(value, axis, [(source, source + steps) for source in range(leading, last)])


def swapped(value, axis, bit):
    count = lax.axis_size(axis)
    return lax.ppermute(value, axis, [(source, source ^ bit) for source in range(count)])


def odd(axis, bit):
    return (lax.axis_index(axis) // bit) % 2 == 1


def tp_bits():
    count = lax.axis_size("tp")
    return [1 << at for at in range(count.bit_length() - 1)]


def tp_sum(value, kind):
    for bit in tp_bits():
        value = value + swapped(value.astype(kind), "tp", bit).astype(F32)
    return value


def tp_gather(value, beside=None):
    pieces = {0: value}
    for bit in reversed(tp_bits()):
        for at in list(pieces):
            pieces[at + bit] = swapped(pieces[at], "tp", bit)
        if beside is not None and bit == tp_bits()[-1]:
            pieces[bit], beside = lax.optimization_barrier((pieces[bit], beside))
    ordered = [pieces[at] for at in range(len(pieces))]
    for bit in tp_bits():
        flip = odd("tp", bit)
        ordered = [
            jnp.where(flip, ordered[at ^ bit], ordered[at]) for at in range(len(ordered))
        ]
    gathered = jnp.concatenate(ordered, axis=-1)
    return gathered if beside is None else (gathered, beside)


def crossing(value):
    rows = value.shape[0] // 2
    return [swapped(value[:rows], "seq", 1), swapped(value[rows:], "seq", 1)]


def tp_scatter(value, beside=None):
    count = lax.axis_size("tp")
    width = value.shape[-1] // count
    parts = [value[..., at * width : (at + 1) * width] for at in range(count)]
    for bit in tp_bits():
        flip = odd("tp", bit)
        pairs = [(parts[2 * at], parts[2 * at + 1]) for at in range(len(parts) // 2)]
        sent = [jnp.where(flip, even, other).astype(LOW) for even, other in pairs]
        mine = [jnp.where(flip, other, even) for even, other in pairs]
        got = [swapped(there, "tp", bit) for there in sent]
        if beside is not None and bit == tp_bits()[-1]:
            got, beside = lax.optimization_barrier((got, beside))
        parts = [here + there.astype(F32) for here, there in zip(mine, got)]
    return parts[0] if beside is None else (parts[0], beside)


def scan_exclusive(decay, value, direction, beside=()):
    count = lax.axis_size("seq")
    states = decay.shape[1]
    outer = None
    step = 1
    while step < count:
        packed = jnp.concatenate([decay, value], axis=1).astype(LOW)
        final = 2 * step >= count
        got = shifted(packed[:, states:] if final else packed, "seq", direction * step)
        if step in beside:
            got, beside[step] = lax.optimization_barrier((got, beside[step]))
        got = got.astype(F32)
        if final:
            got_value = got
        else:
            got_decay, got_value = got[:, :states], got[:, states:]
        if outer is None:
            outer = (got_decay, got_value) if not final else (None, got_value)
        else:
            total, held = outer
            outer = (None if final else total * got_decay, total * got_value + held)
        if not final:
            value = decay * got_value + value
            decay = decay * got_decay
        step *= 2
    return outer[1]


def after(value, *anchors):
    return lax.optimization_barrier((value,) + anchors)[0]


def other_half(value, anchor):
    count = lax.axis_size("seq") // lax.axis_size("tp")
    width = value.shape[-1] // count
    flip = odd("seq", 1)
    blocks = [value[..., at * width : (at + 1) * width] for at in range(count)]
    picked = [jnp.where(flip, blocks[at], blocks[at + 1]) for at in range(0, count, 2)]
    local = jnp.concatenate(picked, axis=-1).reshape(-1, value.shape[-1] // 2)
    return tp_gather(swapped(after(local, anchor), "seq", 1))


def store_products(out_ref, at, count, total):
    parts, block, width = out_ref.shape[0], out_ref.shape[1], out_ref.shape[2] // count
    for part in range(parts):
        rows = total[part * block : (part + 1) * block]
        out_ref[part, :, at * width : (at + 1) * width] = rows.astype(LOW)


def product(left, right):
    return lax.dot_general(left, right, (((0,), (0,)), ((), ())), preferred_element_type=F32)


def pair_kernel(count, side_ref, *refs):
    for at in range(count):
        left, left_other, right, right_other = (ref[...] for ref in refs[4 * at : 4 * at + 4])
        total = product(left, right) + product(left_other, right_other)
        store_products(refs[-1], at, count, total)


def plain_kernel(count, *refs):
    for at in range(count):
        total = product(refs[2 * at][...], refs[2 * at + 1][...])
        store_products(refs[-1], at, count, total)


def product_params(rows, width, total):
    return dict(
        compiler_params=pltpu.CompilerParams(
            dimension_semantics=("arbitrary",), vmem_limit_bytes=56 * 1024 * 1024
        ),
        cost_estimate=pl.CostEstimate(
            flops=2 * rows * width * total, bytes_accessed=4 * rows * total, transcendentals=0
        ),
    )


def own_half(value, other=0):
    count = lax.axis_size("seq")
    width = value.shape[-1] // count
    flip = odd("seq", 1)
    blocks = [value[..., at * width : (at + 1) * width] for at in range(count)]
    picked = [
        jnp.where(flip, blocks[at + 1 - other], blocks[at + other]) for at in range(0, count, 2)
    ]
    return jnp.concatenate(picked, axis=-1)


def pair_products(pieces):
    rows, width = pieces[0][0].shape
    channels = pieces[0][2].shape[1]
    parts = lax.axis_size("seq")
    block = width // parts
    group = max(1, LANES // block)
    side = (lax.axis_index("seq") % 2).astype(jnp.int32).reshape(1)
    specs, operands = [], []
    contiguous = pl.BlockSpec((rows, block * group), lambda at, side: (0, at))
    strided = pl.BlockSpec((rows, block), lambda at, side: (0, 2 * at + side[0]))
    full = pl.BlockSpec((rows, channels), lambda at, side: (0, 0))
    for left, left_other, right, right_other in pieces:
        specs += [strided if group == 1 else contiguous, contiguous, full, full]
        operands += [left if group == 1 else own_half(left), left_other, right, right_other]
    total = len(pieces) * channels
    return pl.pallas_call(
        functools.partial(pair_kernel, len(pieces)),
        grid_spec=pltpu.PrefetchScalarGridSpec(
            num_scalar_prefetch=1,
            grid=(parts // 2 // group,),
            in_specs=specs,
            out_specs=pl.BlockSpec((group, block, total), lambda at, side: (at, 0, 0)),
        ),
        out_shape=jax.ShapeDtypeStruct((parts // 2, block, total), LOW),
        **product_params(rows, width, total),
    )(side, *operands)


def plain_products(pieces):
    rows, width = pieces[0][0].shape
    channels = pieces[0][1].shape[1]
    parts = lax.axis_size("seq")
    block = width // parts
    group = max(1, LANES // block)
    total = len(pieces) * channels
    specs = [
        pl.BlockSpec((rows, block * group), lambda at: (0, at)),
        pl.BlockSpec((rows, channels), lambda at: (0, 0)),
    ] * len(pieces)
    return pl.pallas_call(
        functools.partial(plain_kernel, len(pieces)),
        grid=(parts // group,),
        in_specs=specs,
        out_specs=pl.BlockSpec((group, block, total), lambda at: (at, 0, 0)),
        out_shape=jax.ShapeDtypeStruct((parts, block, total), LOW),
        **product_params(rows, width, total),
    )(*[operand for piece in pieces for operand in piece])


def line_scatter(value):
    count = lax.axis_size("seq")
    groups = [list(range(side, count, 2)) for side in range(2)]
    return lax.psum_scatter(
        value, "seq", scatter_dimension=0, axis_index_groups=groups, tiled=True
    )[0]


def line_task(make):
    anchor = yield
    value = make(anchor)
    long = lax.axis_size("seq") // 2
    place = lax.axis_index("seq") // 2
    pairs = lambda sources, move: [
        (2 * source + side, 2 * (source + move) + side) for source in sources for side in range(2)
    ]
    pick = lambda at: lax.dynamic_index_in_dim(value, jnp.clip(at, 0, long - 1), 0, False)
    right, left = None, None
    for step in range(1, long):
        ahead = pick(place + long - step)
        behind = pick(place - long + step)
        if right is not None:
            right, left, anchor = lax.optimization_barrier((right, left, anchor))
            ahead = (ahead.astype(F32) + right.astype(F32)).astype(LOW)
            behind = (behind.astype(F32) + left.astype(F32)).astype(LOW)
        right = lax.ppermute(ahead, "seq", pairs(range(min(step, long - 1)), 1))
        left = lax.ppermute(behind, "seq", pairs(range(max(long - step, 1), long), -1))
        anchor = yield anchor
    own = pick(place).astype(F32)
    if right is not None:
        right, left, anchor = lax.optimization_barrier((right, left, anchor))
        own = own + right.astype(F32) + left.astype(F32)
    return own, anchor


def advance(tasks, results, anchor):
    if not tasks:
        return anchor
    name, task = tasks[0]
    try:
        return task.send(anchor)
    except StopIteration as ended:
        results[name], anchor = ended.value
        tasks.pop(0)
        return advance(tasks, results, anchor)


def add_task(tasks, name, make):
    task = line_task(make)
    next(task)
    tasks.append((name, task))


def small_task(scattered, summed):
    anchor = yield
    scattered, summed, anchor = lax.optimization_barrier((scattered, summed, anchor))
    bit = 1
    rows, channels = scattered.shape[1:]
    while bit < lax.axis_size("seq"):
        flip = odd("seq", bit)
        parted = scattered.reshape(-1, 2, rows, channels)
        low, high = parted[:, 0], parted[:, 1]
        sent = jnp.where(flip, low, high).astype(LOW).reshape(-1, channels)
        got = swapped(jnp.concatenate([sent, summed.astype(LOW)], axis=0), "seq", bit)
        anchor = yield anchor
        got, anchor = lax.optimization_barrier((got, anchor))
        scattered = jnp.where(flip, high, low).astype(F32)
        scattered = scattered + got[: sent.shape[0]].astype(F32).reshape(scattered.shape)
        summed = summed + got[sent.shape[0] :].astype(F32)
        bit *= 2
    return (scattered[0], summed), anchor


def gated_silu(argument):
    return argument * jax.nn.sigmoid(argument)


def silu_slope(argument):
    logistic = jax.nn.sigmoid(argument)
    return logistic * (1.0 + argument * (1.0 - logistic))


def doc_masks(doc_lengths, doc_offsets, positions):
    before = doc_offsets[:, None, :] <= positions[None, :, None]
    starts = jnp.max(jnp.where(before, doc_offsets[:, None, :], 0), axis=2)
    doc_ends = jnp.max(
        jnp.where(before, doc_offsets[:, None, :] + doc_lengths[:, None, :], 0), axis=2
    )
    return (starts, (positions[None, :] < doc_ends).astype(F32))


def matmul(left, right, dims):
    return jnp.einsum(dims, left, right, preferred_element_type=F32)


def conv_forward(conv_in, previous, conv_weight, conv_bias, tap_masks):
    edge = conv_weight.shape[0] - 1
    rows = conv_in.shape[1]
    extended = jnp.concatenate([previous, conv_in], axis=1).astype(F32)
    running = conv_bias.astype(F32)
    for back in range(edge + 1):
        window = extended[:, edge - back : edge - back + rows]
        running = running + conv_weight[back].astype(F32) * window * tap_masks[back][:, :, None]
    return (extended, running)


def rows_of(value):
    return value.reshape(-1, value.shape[-1])


def forward_layer(hidden, weights, valid_mask, keep_lanes, tap_masks, side, inverse_gain, limit):
    gain, input_w, conv_weight, conv_bias, select_w, step_w, step_bias, skip, out_w = weights
    width = input_w.shape[0]
    scaled = (hidden * gain.astype(F32)).astype(LOW)
    complete, input_w = tp_gather(scaled, input_w)
    unscaled = complete.astype(F32) * inverse_gain
    square_sums = jnp.sum(unscaled * unscaled, axis=2)
    inverse_norm = lax.rsqrt(square_sums / width + norm_epsilon)
    normed_other = None if side is None else other_half(scaled, complete)
    projected = matmul(complete, input_w, "bph,htg->bptg")
    projected = (projected * inverse_norm[:, :, None, None]).astype(LOW)
    conv_in, gate_in = projected[:, :, 0, :], projected[:, :, 1, :]
    edge = conv_weight.shape[0] - 1
    rows = hidden.shape[1]
    previous = shifted(conv_in[:, rows - edge :], "seq", 1)
    extended, conv_out = conv_forward(conv_in, previous, conv_weight, conv_bias, tap_masks)
    conv_act = gated_silu(conv_out).astype(LOW)
    selection = tp_sum(matmul(conv_act, select_w, "mri,ic->mrc"), LOW)
    rank = step_w.shape[0]
    states = (selection.shape[2] - rank) // 2
    low_rank = selection[:, :, :rank].astype(LOW)
    key_state = selection[:, :, rank : rank + states]
    biased = matmul(low_rank, step_w, "mrk,ki->mri") + step_bias
    step_size = jax.nn.softplus(biased)
    key_norm = jnp.sum(key_state * key_state, axis=2)
    rate = step_size / (1.0 + step_size * key_norm[:, :, None])
    side_rows = None if side is None else tp_gather(after(side, rate))
    summary = run_summary(rate, conv_act, selection, keep_lanes, states).astype(F32)
    decay_total, local_state = summary[:, :states], summary[:, states:]
    incoming = scan_exclusive(decay_total, local_state, 1)
    if side is not None:
        incoming, normed_other = lax.optimization_barrier((incoming, normed_other))
    skip_row = skip.astype(F32)[None]
    kept_states, mixed, gated = run_forward(
        rate, conv_act, selection, keep_lanes, gate_in, skip_row, incoming, states, limit
    )
    if side is not None:
        gated, side_rows = lax.optimization_barrier((gated, side_rows))
    finish = lambda rows: hidden + valid_mask[:, :, None] * tp_scatter(
        matmul(rows, out_w, "mri,id->mrd").astype(LOW)
    )
    kept = dict(
        hidden=hidden,
        inverse_norm=inverse_norm,
        complete=complete,
        normed_other=normed_other,
        conv_in=conv_in,
        gate_in=gate_in,
        extended=extended,
        conv_out=conv_out,
        conv_act=conv_act,
        low_rank=low_rank,
        selection=selection,
        biased=biased,
        key_norm=key_norm,
        rate=rate,
        decay_total=decay_total,
        incoming=incoming,
        kept_states=kept_states,
        mixed=mixed,
        gated=gated,
    )
    return (finish, kept, input_w, side_rows)


def backward_layer(
    at,
    grad_new,
    weights,
    kept,
    valid_mask,
    keep_lanes,
    tap_masks,
    tasks,
    results,
    waiting,
    ready,
    gated_other,
):
    gain, input_w, conv_weight, conv_bias, select_w, step_w, step_bias, skip, out_w = weights
    hidden, inverse_norm, rate, selection = (
        kept[name] for name in ("hidden", "inverse_norm", "rate", "selection")
    )
    conv_act = kept["conv_act"]
    width = input_w.shape[0]
    rank = step_w.shape[0]
    states = (selection.shape[2] - rank) // 2
    skip_row = skip.astype(F32)[None]
    first = waiting is not None
    if ready is None:
        branch_local = (grad_new * valid_mask[:, :, None]).astype(LOW)
        branch_rows, last = tp_gather(branch_local, waiting[3][1])
        waiting = waiting[:3] + (jnp.concatenate([waiting[3][0], last], axis=0),)
    else:
        branch_rows = ready
    grad_gated = matmul(branch_rows, out_w, "mrd,id->mri")
    gate_in = kept["gate_in"].astype(F32)
    grad_mixed = grad_gated * gated_silu(gate_in)
    inverse = inverse_norm[:, :, None]
    grad_gate = grad_gated * kept["mixed"].astype(F32) * silu_slope(gate_in) * inverse
    grad_gate = grad_gate.astype(LOW)
    act_float = conv_act.astype(F32)
    skip_grad = jnp.sum(grad_mixed * act_float, axis=(0, 1))
    normed = rows_of(kept["complete"])
    local_carry = run_adjoint(rate, grad_mixed, selection, keep_lanes, states)
    if first:
        branch_other = swapped(own_half(rows_of(branch_rows), 1), "seq", 1)
        inside = {1: pair_products([waiting]), 4: branch_other}
        carried = scan_exclusive(kept["decay_total"], local_carry.astype(F32), -1, inside)
        carried, results[("early", at + 1)] = lax.optimization_barrier(
            (carried, results[("early", at + 1)])
        )
        results[("conv", at + 1)] = line_scatter(inside[1]).astype(F32)
    else:
        local_carry, gated_other = lax.optimization_barrier((local_carry, gated_other))
        carried = scan_exclusive(kept["decay_total"], local_carry.astype(F32), -1)
        partial = plain_products(
            [
                (normed, rows_of(grad_gate)),
                (rows_of(branch_rows), rows_of(kept["gated"])),
            ]
        )
        carried, partial = lax.optimization_barrier((carried, partial))
        results[("early", at)] = lax.psum_scatter(
            partial, "seq", scatter_dimension=0, tiled=True
        )[0]
    grad_rate, grad_act, sums = run_backward(
        rate,
        conv_act,
        grad_mixed,
        selection,
        keep_lanes,
        skip_row,
        kept["kept_states"],
        kept["incoming"],
        carried,
        states,
        2 * VMEM_BYTES,
    )
    if first:
        gate_other = swapped(after(rows_of(grad_gate), carried), "seq", 1)
        grad_rate, gate_other = lax.optimization_barrier((grad_rate, gate_other))
        partial = pair_products(
            [
                (normed, kept["normed_other"], rows_of(grad_gate), gate_other),
                (rows_of(branch_rows), inside.get(4, branch_other), rows_of(kept["gated"]), gated_other),
            ]
        )
    else:
        normed_other = swapped(own_half(normed, 1), "seq", 1)
        grad_rate, normed_other = lax.optimization_barrier((grad_rate, normed_other))
    denominator = 1.0 + jax.nn.softplus(kept["biased"]) * kept["key_norm"][:, :, None]
    grad_step = grad_rate / (denominator * denominator)
    grad_norm_key = -jnp.sum(grad_rate * rate * rate, axis=2)
    grad_pre = grad_step * jax.nn.sigmoid(kept["biased"])
    stepbias_grad = jnp.sum(grad_pre, axis=(0, 1))
    grad_pre_low = grad_pre.astype(LOW)
    step_grad = matmul(kept["low_rank"], grad_pre_low, "mrk,mri->ki")
    padded = jnp.pad(step_w, ((0, 2 * states), (0, 0)))
    lanes = jnp.arange(selection.shape[2], dtype=jnp.int32)
    is_key = ((lanes >= rank) & (lanes < rank + states)).astype(F32)
    grad_selection = matmul(grad_pre_low, padded, "mri,ki->mrk") + sums
    grad_selection = grad_selection + 2.0 * is_key * selection * grad_norm_key[:, :, None]
    grad_selection = tp_sum(grad_selection, LOW)
    grad_selection = grad_selection.astype(LOW)
    if first:
        grad_selection, partial = lax.optimization_barrier((grad_selection, partial))
        results[("early", at)] = line_scatter(partial)
    select_full = matmul(grad_selection, conv_act, "mrc,mri->ci")
    grad_act = grad_act + matmul(grad_selection, select_w, "mrc,ic->mri")
    grad_conv = grad_act * silu_slope(kept["conv_out"])
    convbias_grad = jnp.sum(grad_conv, axis=(0, 1))
    edge = conv_weight.shape[0] - 1
    rows = grad_conv.shape[1]
    extended = kept["extended"]
    tap_grads = []
    grad_extended = jnp.zeros(extended.shape, F32)
    for back in range(edge + 1):
        masked = grad_conv * tap_masks[back][:, :, None]
        tap_grads.append(jnp.sum(masked * extended[:, edge - back : edge - back + rows], axis=(0, 1)))
        grad_extended = grad_extended + jnp.pad(
            masked * conv_weight[back].astype(F32), ((0, 0), (edge - back, back), (0, 0))
        )
    returned = shifted(grad_extended[:, :edge], "seq", -1)
    grad_conv_in = grad_extended[:, edge:] + jnp.pad(
        returned, ((0, 0), (rows - edge, 0), (0, 0))
    )
    grad_conv_in = (grad_conv_in * inverse).astype(LOW)
    conv_other = crossing(rows_of(grad_conv_in))
    if first:
        normed_other = kept["normed_other"]
    grad_projected = jnp.stack([grad_conv_in, grad_gate], axis=2)
    grad_normed = matmul(grad_projected, input_w, "bptg,htg->bph").astype(LOW)
    if first:
        grad_normed, conv_first = lax.optimization_barrier((grad_normed, conv_other[0]))
        grad_normed, conv_last = tp_scatter(grad_normed, conv_other[1])
        conv_other = jnp.concatenate([conv_first, conv_last], axis=0)
    else:
        grad_normed, conv_first = tp_scatter(grad_normed, conv_other[0])
        conv_other = (conv_first, conv_other[1])
    grad_normed = grad_normed.astype(F32)
    conv_piece = (normed, normed_other, rows_of(grad_conv_in), conv_other)
    inner = tp_sum(
        jnp.sum(
            grad_conv_in.astype(F32) * kept["conv_in"].astype(F32)
            + grad_gate.astype(F32) * gate_in,
            axis=2,
        ),
        F32,
    )
    gain_grad = jnp.sum(grad_normed * hidden, axis=(0, 1))
    grad_hidden = (
        grad_new
        + gain.astype(F32) * grad_normed
        - hidden * (inverse_norm * inner / width)[:, :, None]
    )
    count = lax.axis_size("seq")
    scattered = jnp.stack([select_full[:rank], step_grad], axis=0)
    scattered = scattered.reshape(2, count, rank // count, -1).swapaxes(0, 1)
    channels = conv_act.shape[2]
    summed = jnp.concatenate(
        [
            jnp.stack(tap_grads + [convbias_grad, stepbias_grad, skip_grad], axis=0),
            select_full[rank:],
            jnp.pad(gain_grad, (0, channels - gain_grad.shape[0]))[None],
        ],
        axis=0,
    )
    return (grad_hidden, conv_piece, gated_other, scattered, summed)


def on_device(
    tokens,
    norm_gain,
    input_weight,
    conv_weight,
    conv_bias,
    select_weight,
    step_weight,
    step_bias,
    skip_gain,
    out_weight,
    cotangent,
    doc_lengths,
    doc_offsets,
):
    rows = tokens.shape[1]
    positions = lax.axis_index("seq") * rows + jnp.arange(rows, dtype=jnp.int32)
    starts, valid_mask = doc_masks(doc_lengths, doc_offsets, positions)
    keep_mask = (positions[None, :] != starts).astype(F32)
    tap_masks = [
        (positions[None, :] - back >= starts).astype(F32) for back in range(conv_weight.shape[1])
    ]
    layers = input_weight.shape[0]
    keep_lanes = jnp.broadcast_to(keep_mask[:, :, None], keep_mask.shape + (LANES,))
    small = (conv_weight, conv_bias, select_weight, step_weight, step_bias, skip_gain, out_weight)
    shared = [tuple(member[at] for member in small) for at in range(layers)]
    hidden = tokens.astype(F32)
    grad = cotangent.astype(F32)
    side = (grad * valid_mask[:, :, None]).astype(LOW)
    inverse_gains = 1.0 / tp_gather(norm_gain.astype(F32))
    saved, inputs, ready = [], [None] * layers, None
    for at in range(layers):
        own = after(input_weight[at], hidden)
        finish, kept, inputs[at], extra = forward_layer(
            hidden,
            (norm_gain[at], own) + shared[at],
            valid_mask,
            keep_lanes,
            tap_masks,
            side if at == 0 else None,
            inverse_gains[at],
            2 * VMEM_BYTES,
        )
        ready = extra if at == 0 else ready
        saved.append(kept)
        if at + 1 < layers:
            hidden = finish(kept["gated"])
    tasks, results, waiting = [], {}, None
    passing = swapped(rows_of(saved[0]["gated"]), "seq", 1)
    scattered, summed = [None] * layers, [None] * layers
    for at in reversed(range(layers)):
        grad, waiting, passing, scattered[at], summed[at] = backward_layer(
            at,
            grad,
            (norm_gain[at], inputs[at]) + shared[at],
            saved[at],
            valid_mask,
            keep_lanes,
            tap_masks,
            tasks,
            results,
            waiting,
            ready if waiting is None else None,
            passing,
        )
    layer_out = finish(after(saved[-1]["gated"], grad)).astype(LOW)
    piece = waiting
    add_task(tasks, ("conv", 0), lambda anchor: pair_products([piece]))
    rank = step_weight.shape[1]
    count = lax.axis_size("seq")
    packed = jnp.stack(scattered, axis=1).reshape(count, -1, out_weight.shape[1])
    small = small_task(packed, jnp.concatenate(summed, axis=0))
    next(small)
    extra = [("small", small)]
    while tasks or extra:
        grad = advance(tasks, results, grad)
        grad = advance(extra, results, grad)
    scattered, summed = results["small"]
    scattered = scattered.reshape(layers, 2, rank // count, -1)
    summed = summed.reshape(layers, -1, summed.shape[1])
    channels = out_weight.shape[1]
    parts = [
        [results[("early", at)][:, piece * channels : (piece + 1) * channels] for piece in range(2)]
        for at in range(layers)
    ]
    conv_parts = [results[("conv", at)] for at in range(layers)]
    gate_parts = [parts[at][0].astype(F32) for at in range(layers)]
    out_parts = [parts[at][1].astype(F32) for at in range(layers)]
    edge = conv_weight.shape[1]
    blank = [jnp.zeros_like(conv_parts[0])] + conv_parts[1:]
    inweight_grad = jnp.stack(
        [jnp.stack([conv, gate], axis=1) for conv, gate in zip(blank, gate_parts)], axis=0
    )
    inweight_grad = lax.dynamic_update_slice(
        inweight_grad, conv_parts[0][None, :, None, :], (0, 0, 0, 0)
    )
    return (
        layer_out,
        grad.astype(LOW),
        summed[:, -1, : norm_gain.shape[1]],
        inweight_grad,
        summed[:, :edge],
        summed[:, edge],
        jnp.swapaxes(scattered[:, 0], 1, 2),
        jnp.swapaxes(summed[:, edge + 3 : -1], 1, 2),
        scattered[:, 1],
        summed[:, edge + 1],
        summed[:, edge + 2],
        jnp.swapaxes(jnp.stack(out_parts, axis=0), 1, 2),
    )


def solution(mesh):
    placed = (
        P(None, "seq", "tp"),
        P(None, "tp"),
        P(None, None, None, "tp"),
        P(None, None, "tp"),
        P(None, "tp"),
        P(None, "tp", None),
        P(None, None, "tp"),
        P(None, "tp"),
        P(None, "tp"),
        P(None, "tp", None),
        P(None, "seq", "tp"),
        P(),
        P(),
    )
    return jax.shard_map(
        on_device,
        mesh=mesh,
        in_specs=placed,
        out_specs=(
            P(None, "seq", "tp"),
            P(None, "seq", "tp"),
            P(None, "tp"),
            P(None, "seq", None, "tp"),
            P(None, None, "tp"),
            P(None, "tp"),
            P(None, "tp", "seq"),
            P(None, "tp", None),
            P(None, "seq", "tp"),
            P(None, "tp"),
            P(None, "tp"),
            P(None, "tp", "seq"),
        ),
        check_vma=False,
    )
```

```python
import functools
import jax
import jax.numpy as jnp
import numpy as np
from jax import lax
from jax.experimental import pallas as pl
from jax.experimental.pallas import tpu as pltpu
from jax.sharding import PartitionSpec as P

CH = 16
LANES = 128
VMEM_BYTES = 27 * 1024 * 1024
BLOCK = 128
norm_epsilon = 1e-05
F32 = jnp.float32
LOW = jnp.bfloat16


def positions_of(shape, dimension):
    return lax.broadcasted_iota(jnp.int32, shape, dimension)


def fill_tables(states, pick_ref, diagonal_ref, fold_ref=None, own_ref=None):
    low, bits = states - 1, states.bit_length() - 1
    rows, lanes = positions_of(pick_ref.shape, 0), positions_of(pick_ref.shape, 1)
    pick_ref[...] = jnp.where(rows == (lanes & low), 1.0, 0.0).astype(LOW)
    diagonal_ref[...] = jnp.where(rows == (lanes >> bits), 1.0, 0.0).astype(F32)
    if fold_ref is not None:
        rows, lanes = positions_of(fold_ref.shape, 0), positions_of(fold_ref.shape, 1)
        same = (rows >> (LANES.bit_length() - 1)) == (lanes >> bits)
        fold_ref[...] = jnp.where(same, 1.0, 0.0).astype(LOW)
        rows, lanes = positions_of(own_ref.shape, 0), positions_of(own_ref.shape, 1)
        own_ref[...] = jnp.where((rows & low) == (lanes & low), 1.0, 0.0).astype(F32)


def dot(left, right):
    return jnp.dot(left, right, preferred_element_type=F32)


def spread_table(sel_ref, keep_ref, rows, states):
    start = sel_ref.shape[1] - 2 * states
    turned = sel_ref[rows, start:].T
    key, query = turned[:states], turned[states:]
    keep = keep_ref[rows, :].T[:states]
    return jnp.concatenate([key, keep * key * key, keep, query], axis=0)


def spread_rows(table, row, states):
    wide = jnp.broadcast_to(table[:, row : row + 1], (table.shape[0], LANES))
    return [wide[at : at + states] for at in range(0, 4 * states, states)]


def expanded(value, pick_ref, diagonal_ref):
    return (dot(value.astype(LOW), pick_ref[...]) * diagonal_ref[...]).astype(LOW)


def groups(width):
    return [slice(at, at + LANES) for at in range(0, width, LANES)]


def row_of(ref, at, lanes):
    return ref[at : at + 1, lanes]


def summary_kernel(
    states, r_ref, act_ref, sel_ref, keep_ref, out_ref, *scratch
):
    feed_refs = scratch[0:2]
    decay_ref, state_ref = scratch[2:]
    step = pl.program_id(1)
    r_ref, act_ref, sel_ref, keep_ref = r_ref.at[0], act_ref.at[0], sel_ref.at[0], keep_ref.at[0]
    count = r_ref.shape[0] // CH
    parts = groups(r_ref.shape[1])

    @pl.when(step == 0)
    def _():
        decay_ref[...] = jnp.ones_like(decay_ref)
        state_ref[...] = jnp.zeros_like(state_ref)

    def prepare(index, which):
        rows = pl.ds(pl.multiple_of(index * CH, CH), CH)
        feed_refs[which][...] = r_ref[rows, :] * act_ref[rows, :].astype(F32)

    def process(index, which, decays, values):
        base = pl.multiple_of(index * CH, CH)
        rates = r_ref.at[pl.ds(base, CH)]
        table, feeds = spread_table(sel_ref, keep_ref, pl.ds(base, CH), states), feed_refs[which]
        for row in range(CH):
            mine = slice(row * states, (row + 1) * states)
            key, square, keep, _ = spread_rows(table, row, states)
            for at, lanes in enumerate(parts):
                decay = keep - row_of(rates, row, lanes) * square
                values[at] = decay * values[at] + row_of(feeds, row, lanes) * key
                decays[at] = decays[at] * decay

    prepare(0, 0)

    def pair(turn, carry):
        decays, values = list(carry[0]), list(carry[1])
        prepare(2 * turn + 1, 1)
        process(2 * turn, 0, decays, values)
        prepare(jnp.minimum(2 * turn + 2, count - 1), 0)
        process(2 * turn + 1, 1, decays, values)
        return (tuple(decays), tuple(values))

    start = (
        tuple(decay_ref[:, lanes] for lanes in parts),
        tuple(state_ref[:, lanes] for lanes in parts),
    )
    decays, values = lax.fori_loop(0, count // 2, pair, start)
    for at, lanes in enumerate(parts):
        decay_ref[:, lanes] = decays[at]
        state_ref[:, lanes] = values[at]

    @pl.when(step == pl.num_programs(1) - 1)
    def _():
        out_ref[0, :states] = decay_ref[...].astype(out_ref.dtype)
        out_ref[0, states:] = state_ref[...].astype(out_ref.dtype)


def forward_kernel(
    states,
    r_ref,
    act_ref,
    sel_ref,
    keep_ref,
    gate_ref,
    skip_ref,
    in_ref,
    states_ref,
    mixed_ref,
    gated_ref,
    *scratch,
):
    feed_refs, value_refs = scratch[0:2], scratch[2:4]
    state_ref, pick_ref, diagonal_ref = scratch[4:]
    fill_tables(states, pick_ref, diagonal_ref)
    step = pl.program_id(1)
    r_ref, act_ref, sel_ref, gate_ref = r_ref.at[0], act_ref.at[0], sel_ref.at[0], gate_ref.at[0]
    keep_ref = keep_ref.at[0]
    states_ref, mixed_ref, gated_ref = states_ref.at[0], mixed_ref.at[0], gated_ref.at[0]
    count = r_ref.shape[0] // CH
    parts = groups(r_ref.shape[1])

    @pl.when(step == 0)
    def _():
        state_ref[...] = in_ref[0].astype(F32)

    def prepare(index, which):
        rows = pl.ds(pl.multiple_of(index * CH, CH), CH)
        feed_refs[which][...] = r_ref[rows, :] * act_ref[rows, :].astype(F32)

    def process(index, which, values):
        base = pl.multiple_of(index * CH, CH)
        rates = r_ref.at[pl.ds(base, CH)]
        first = pl.multiple_of(index * (CH * states), CH * states)
        table, feeds = spread_table(sel_ref, keep_ref, pl.ds(base, CH), states), feed_refs[which]
        for row in range(CH):
            mine = slice(row * states, (row + 1) * states)
            key, square, keep, _ = spread_rows(table, row, states)
            for at, lanes in enumerate(parts):
                decay = keep - row_of(rates, row, lanes) * square
                values[at] = decay * values[at] + row_of(feeds, row, lanes) * key
                low = values[at].astype(LOW)
                states_ref[pl.ds(first + row * states, states), lanes] = low
                value_refs[which][mine, lanes] = low

    def finish(index, which):
        rows = pl.ds(pl.multiple_of(index * CH, CH), CH)
        query = expanded(sel_ref[rows, sel_ref.shape[1] - states :], pick_ref, diagonal_ref)
        recurrent = dot(query, value_refs[which][...])
        mixed = recurrent + skip_ref[...] * act_ref[rows, :].astype(F32)
        gate = gate_ref[rows, :].astype(F32)
        mixed_ref[rows, :] = mixed.astype(mixed_ref.dtype)
        gated_ref[rows, :] = (mixed * gate / (1.0 + jnp.exp(-gate))).astype(gated_ref.dtype)

    prepare(0, 0)

    def pair(turn, carry):
        values = list(carry)
        finish(jnp.maximum(2 * turn - 1, 0), 1)
        prepare(2 * turn + 1, 1)
        process(2 * turn, 0, values)
        finish(2 * turn, 0)
        prepare(jnp.minimum(2 * turn + 2, count - 1), 0)
        process(2 * turn + 1, 1, values)
        return tuple(values)

    values = lax.fori_loop(0, count // 2, pair, tuple(state_ref[:, lanes] for lanes in parts))
    finish(count - 1, 1)
    for at, lanes in enumerate(parts):
        state_ref[:, lanes] = values[at]


def adjoint_kernel(
    states, r_ref, gm_ref, sel_ref, keep_ref, out_ref, *scratch
):
    (carry_ref,) = scratch
    step = pl.program_id(1)
    r_ref, gm_ref, sel_ref, keep_ref = r_ref.at[0], gm_ref.at[0], sel_ref.at[0], keep_ref.at[0]
    count = r_ref.shape[0] // CH
    parts = groups(r_ref.shape[1])

    @pl.when(step == 0)
    def _():
        carry_ref[...] = jnp.zeros_like(carry_ref)


    def process(index, which, values):
        base = pl.multiple_of(index * CH, CH)
        rates = r_ref.at[pl.ds(base, CH)]
        grads = gm_ref.at[pl.ds(base, CH)]
        table = spread_table(sel_ref, keep_ref, pl.ds(base, CH), states)
        for row in reversed(range(CH)):
            mine = slice(row * states, (row + 1) * states)
            _, square, keep, query = spread_rows(table, row, states)
            for at, lanes in enumerate(parts):
                adjoint = query * row_of(grads, row, lanes) + values[at]
                values[at] = (keep - row_of(rates, row, lanes) * square) * adjoint


    def pair(turn, carry):
        values = list(carry)
        index = count - 1 - 2 * turn
        process(index, 0, values)
        process(index - 1, 1, values)
        return tuple(values)

    values = lax.fori_loop(0, count // 2, pair, tuple(carry_ref[:, lanes] for lanes in parts))
    for at, lanes in enumerate(parts):
        carry_ref[:, lanes] = values[at]

    @pl.when(step == pl.num_programs(1) - 1)
    def _():
        out_ref[0] = carry_ref[...].astype(out_ref.dtype)


def backward_kernel(
    states,
    r_ref,
    act_ref,
    gm_ref,
    sel_ref,
    keep_ref,
    skip_ref,
    states_ref,
    before_ref,
    in_ref,
    carry_in_ref,
    rate_ref,
    gact_ref,
    sums_ref,
    *scratch,
):
    feed_refs, adjoint_refs, product_refs, part_refs = (
        scratch[2 * at : 2 * at + 2] for at in range(4)
    )
    first_ref, carry_ref, pick_ref, diagonal_ref, fold_ref, fold_own_ref = scratch[8:]
    fill_tables(states, pick_ref, diagonal_ref, fold_ref, fold_own_ref)
    step = pl.program_id(1)
    last = pl.num_programs(1) - 1
    r_ref, act_ref, gm_ref, sel_ref = r_ref.at[0], act_ref.at[0], gm_ref.at[0], sel_ref.at[0]
    keep_ref = keep_ref.at[0]
    states_ref, rate_ref, gact_ref, sums_ref = (
        states_ref.at[0],
        rate_ref.at[0],
        gact_ref.at[0],
        sums_ref.at[0],
    )
    count = r_ref.shape[0] // CH
    parts = groups(r_ref.shape[1])

    @pl.when(step == 0)
    def _():
        carry_ref[...] = carry_in_ref[0].astype(F32)

    @pl.when(step == last)
    def _():
        first_ref[...] = in_ref[0].astype(LOW)

    @pl.when(step != last)
    def _():
        first_ref[...] = before_ref[0]

    def prepare(index, which):
        rows = pl.ds(pl.multiple_of(index * CH, CH), CH)
        feed_refs[which][...] = r_ref[rows, :] * act_ref[rows, :].astype(F32)

    def process(index, which, values, held):
        base = pl.multiple_of(index * CH, CH)
        rates = r_ref.at[pl.ds(base, CH)]
        grads = gm_ref.at[pl.ds(base, CH)]
        first = pl.multiple_of(index * (CH * states), CH * states)
        table, feeds = spread_table(sel_ref, keep_ref, pl.ds(base, CH), states), feed_refs[which]
        for row in reversed(range(CH)):
            mine = slice(row * states, (row + 1) * states)
            _, square, keep, query = spread_rows(table, row, states)
            sums = [None, None, None]
            for at, lanes in enumerate(parts):
                rate = row_of(rates, row, lanes)
                grad = row_of(grads, row, lanes)
                if row:
                    previous = states_ref[pl.ds(first + (row - 1) * states, states), lanes]
                else:
                    before = pl.multiple_of(jnp.maximum(first - states, 0), states)
                    previous = jnp.where(
                        index == 0, first_ref[:, lanes], states_ref[pl.ds(before, states), lanes]
                    )
                previous = previous.astype(F32)
                adjoint = query * grad + values[at]
                product = adjoint * previous
                values[at] = (keep - rate * square) * adjoint
                adjoint_refs[which][mine, lanes] = adjoint.astype(LOW)
                product_refs[which][mine, lanes] = product.astype(LOW)
                terms = (adjoint * row_of(feeds, row, lanes), product * rate, held[at] * grad)
                for kind, term in enumerate(terms):
                    sums[kind] = term if sums[kind] is None else sums[kind] + term
                held[at] = previous
            for kind in range(3):
                part_refs[which][mine, kind * LANES : (kind + 1) * LANES] = sums[kind].astype(LOW)

    def finish(index, which):
        rows = pl.ds(pl.multiple_of(index * CH, CH), CH)
        start = sel_ref.shape[1] - 2 * states
        key = sel_ref[rows, start : start + states]
        kept_key = keep_ref[rows, :states] * key
        keys = expanded(key, pick_ref, diagonal_ref)
        squares = expanded(kept_key * key, pick_ref, diagonal_ref)
        through_key = dot(keys, adjoint_refs[which][...])
        through_decay = dot(squares, product_refs[which][...])
        rate_ref[rows, :] = act_ref[rows, :].astype(F32) * through_key - through_decay
        gact_ref[rows, :] = r_ref[rows, :] * through_key + skip_ref[...] * gm_ref[rows, :]
        folded = dot(part_refs[which][...], fold_ref[...]) * fold_own_ref[...]
        high = folded.astype(LOW)
        rest = (folded - high.astype(F32)).astype(LOW)
        gather = diagonal_ref[...].astype(LOW)
        total = dot(gather, high) + dot(gather, rest)
        grad_key = total[:, :states] - 2.0 * kept_key * total[:, states : 2 * states]
        sums_ref[rows, :start] = jnp.zeros((CH, start), F32)
        sums_ref[rows, start : start + states] = grad_key
        sums_ref[rows, start + states :] = total[:, 2 * states : 3 * states]

    prepare(count - 1, 0)

    def pair(turn, carry):
        values, held = list(carry[0]), list(carry[1])
        index = count - 1 - 2 * turn
        finish(jnp.minimum(index + 1, count - 1), 1)
        prepare(index - 1, 1)
        process(index, 0, values, held)
        finish(index, 0)
        prepare(jnp.maximum(index - 2, 0), 0)
        process(index - 1, 1, values, held)
        return (tuple(values), tuple(held))

    tail = pl.ds((count * CH - 1) * states, states)
    start = (
        tuple(carry_ref[:, lanes] for lanes in parts),
        tuple(states_ref[tail, lanes].astype(F32) for lanes in parts),
    )
    values, _ = lax.fori_loop(0, count // 2, pair, start)
    finish(0, 1)
    for at, lanes in enumerate(parts):
        carry_ref[:, lanes] = values[at]


def plan(rate):
    batch, rows, channels = rate.shape
    block = BLOCK if rows % BLOCK == 0 else rows
    return batch, rows, channels, block, (batch, rows // block)


def cost(rate, states, work):
    size = rate.shape[0] * rate.shape[1] * rate.shape[2] * states
    return pl.CostEstimate(flops=size * work, bytes_accessed=size * 2, transcendentals=0)


def params(limit=VMEM_BYTES):
    return pltpu.CompilerParams(
        dimension_semantics=("arbitrary", "arbitrary"), vmem_limit_bytes=limit
    )


def whole(value):
    return pl.BlockSpec(value.shape, lambda m, b: (0,) * value.ndim)


def table_shapes(states):
    return [
        pltpu.VMEM((states, CH * states), LOW),
        pltpu.VMEM((CH, CH * states), F32),
        pltpu.VMEM((3 * LANES, LANES), LOW),
        pltpu.VMEM((CH * states, LANES), F32),
    ]


def run_summary(rate, act, sel, keep, states):
    batch, rows, channels, block, grid = plan(rate)
    part = pl.BlockSpec((1, block, channels), lambda m, b: (m, b, 0))
    narrow = pl.BlockSpec((1, block, sel.shape[2]), lambda m, b: (m, b, 0))
    marks = pl.BlockSpec((1, block, LANES), lambda m, b: (m, b, 0))
    return pl.pallas_call(
        functools.partial(summary_kernel, states),
        grid=grid,
        in_specs=[part, part, narrow, marks],
        out_specs=pl.BlockSpec((1, 2 * states, channels), lambda m, b: (m, 0, 0)),
        out_shape=jax.ShapeDtypeStruct((batch, 2 * states, channels), LOW),
        scratch_shapes=[pltpu.VMEM((CH, channels), F32)] * 2
        + [pltpu.VMEM((states, channels), F32)] * 2,
        compiler_params=params(),
        cost_estimate=cost(rate, states, 6),
    )(rate, act, sel, keep)


def run_forward(rate, act, sel, keep, gate, skip, incoming, states, limit):
    batch, rows, channels, block, grid = plan(rate)
    part = pl.BlockSpec((1, block, channels), lambda m, b: (m, b, 0))
    narrow = pl.BlockSpec((1, block, sel.shape[2]), lambda m, b: (m, b, 0))
    marks = pl.BlockSpec((1, block, LANES), lambda m, b: (m, b, 0))
    edge = pl.BlockSpec((1, states, channels), lambda m, b: (m, 0, 0))
    return pl.pallas_call(
        functools.partial(forward_kernel, states),
        grid=grid,
        in_specs=[part, part, narrow, marks, part, whole(skip), edge],
        out_specs=[
            pl.BlockSpec((1, block * states, channels), lambda m, b: (m, b, 0)),
            part,
            part,
        ],
        out_shape=[
            jax.ShapeDtypeStruct((batch, rows * states, channels), LOW),
            jax.ShapeDtypeStruct((batch, rows, channels), LOW),
            jax.ShapeDtypeStruct((batch, rows, channels), LOW),
        ],
        scratch_shapes=[pltpu.VMEM((CH, channels), F32)] * 2
        + [pltpu.VMEM((CH * states, channels), LOW)] * 2
        + [pltpu.VMEM((states, channels), F32)]
        + table_shapes(states)[:2],
        compiler_params=params(limit),
        cost_estimate=cost(rate, states, 8),
    )(rate, act, sel, keep, gate, skip, incoming)


def run_adjoint(rate, grad_mixed, sel, keep, states):
    batch, rows, channels, block, grid = plan(rate)
    final = rows // block - 1
    part = pl.BlockSpec((1, block, channels), lambda m, b: (m, final - b, 0))
    narrow = pl.BlockSpec((1, block, sel.shape[2]), lambda m, b: (m, final - b, 0))
    marks = pl.BlockSpec((1, block, LANES), lambda m, b: (m, final - b, 0))
    return pl.pallas_call(
        functools.partial(adjoint_kernel, states),
        grid=grid,
        in_specs=[part, part, narrow, marks],
        out_specs=pl.BlockSpec((1, states, channels), lambda m, b: (m, 0, 0)),
        out_shape=jax.ShapeDtypeStruct((batch, states, channels), LOW),
        scratch_shapes=[pltpu.VMEM((states, channels), F32)],
        compiler_params=params(),
        cost_estimate=cost(rate, states, 5),
    )(rate, grad_mixed, sel, keep)


def run_backward(
    rate, act, grad_mixed, sel, keep, skip, kept_states, incoming, carry, states, limit
):
    batch, rows, channels, block, grid = plan(rate)
    final = rows // block - 1
    part = pl.BlockSpec((1, block, channels), lambda m, b: (m, final - b, 0))
    narrow = pl.BlockSpec((1, block, sel.shape[2]), lambda m, b: (m, final - b, 0))
    marks = pl.BlockSpec((1, block, LANES), lambda m, b: (m, final - b, 0))
    edge = pl.BlockSpec((1, states, channels), lambda m, b: (m, 0, 0))
    return pl.pallas_call(
        functools.partial(backward_kernel, states),
        grid=grid,
        in_specs=[
            part,
            part,
            part,
            narrow,
            marks,
            whole(skip),
            pl.BlockSpec((1, block * states, channels), lambda m, b: (m, final - b, 0)),
            pl.BlockSpec(
                (1, states, channels),
                lambda m, b: (m, jnp.maximum((final - b) * block - 1, 0), 0),
            ),
            edge,
            edge,
        ]
       ,
        out_specs=[part, part, narrow],
        out_shape=[
            jax.ShapeDtypeStruct((batch, rows, channels), F32),
            jax.ShapeDtypeStruct((batch, rows, channels), F32),
            jax.ShapeDtypeStruct((batch, rows, sel.shape[2]), F32),
        ],
        scratch_shapes=[pltpu.VMEM((CH, channels), F32)] * 2
        + [pltpu.VMEM((CH * states, channels), LOW)] * 4
        + [pltpu.VMEM((CH * states, 3 * LANES), LOW)] * 2
        + [pltpu.VMEM((states, channels), LOW), pltpu.VMEM((states, channels), F32)]
        + table_shapes(states),
        compiler_params=params(limit),
        cost_estimate=cost(rate, states, 16),
    )(rate, act, grad_mixed, sel, keep, skip, kept_states, kept_states, incoming, carry)


def shifted(value, axis, steps):
    count = lax.axis_size(axis)
    leading, last = (max(0, -steps), min(count, count - steps))
    return lax.ppermute(value, axis, [(source, source + steps) for source in range(leading, last)])


def swapped(value, axis, bit):
    count = lax.axis_size(axis)
    return lax.ppermute(value, axis, [(source, source ^ bit) for source in range(count)])


def odd(axis, bit):
    return (lax.axis_index(axis) // bit) % 2 == 1


def tp_bits():
    count = lax.axis_size("tp")
    return [1 << at for at in range(count.bit_length() - 1)]


def tp_sum(value, kind):
    for bit in tp_bits():
        value = value + swapped(value.astype(kind), "tp", bit).astype(F32)
    return value


def tp_gather(value, beside=None):
    pieces = {0: value}
    for bit in reversed(tp_bits()):
        for at in list(pieces):
            pieces[at + bit] = swapped(pieces[at], "tp", bit)
        if beside is not None and bit == tp_bits()[-1]:
            pieces[bit], beside = lax.optimization_barrier((pieces[bit], beside))
    ordered = [pieces[at] for at in range(len(pieces))]
    for bit in tp_bits():
        flip = odd("tp", bit)
        ordered = [
            jnp.where(flip, ordered[at ^ bit], ordered[at]) for at in range(len(ordered))
        ]
    gathered = jnp.concatenate(ordered, axis=-1)
    return gathered if beside is None else (gathered, beside)


def crossing(value):
    rows = value.shape[0] // 2
    return [swapped(value[:rows], "seq", 1), swapped(value[rows:], "seq", 1)]


def tp_scatter(value, beside=None):
    count = lax.axis_size("tp")
    width = value.shape[-1] // count
    parts = [value[..., at * width : (at + 1) * width] for at in range(count)]
    for bit in tp_bits():
        flip = odd("tp", bit)
        pairs = [(parts[2 * at], parts[2 * at + 1]) for at in range(len(parts) // 2)]
        sent = [jnp.where(flip, even, other).astype(LOW) for even, other in pairs]
        mine = [jnp.where(flip, other, even) for even, other in pairs]
        got = [swapped(there, "tp", bit) for there in sent]
        if beside is not None and bit == tp_bits()[-1]:
            got, beside = lax.optimization_barrier((got, beside))
        parts = [here + there.astype(F32) for here, there in zip(mine, got)]
    return parts[0] if beside is None else (parts[0], beside)


def scan_exclusive(decay, value, direction, beside=()):
    count = lax.axis_size("seq")
    states = decay.shape[1]
    outer = None
    step = 1
    while step < count:
        packed = jnp.concatenate([decay, value], axis=1).astype(LOW)
        final = 2 * step >= count
        got = shifted(packed[:, states:] if final else packed, "seq", direction * step)
        if step in beside:
            got, beside[step] = lax.optimization_barrier((got, beside[step]))
        got = got.astype(F32)
        if final:
            got_value = got
        else:
            got_decay, got_value = got[:, :states], got[:, states:]
        if outer is None:
            outer = (got_decay, got_value) if not final else (None, got_value)
        else:
            total, held = outer
            outer = (None if final else total * got_decay, total * got_value + held)
        if not final:
            value = decay * got_value + value
            decay = decay * got_decay
        step *= 2
    return outer[1]


def after(value, *anchors):
    return lax.optimization_barrier((value,) + anchors)[0]


def other_half(value, anchor):
    count = lax.axis_size("seq") // lax.axis_size("tp")
    width = value.shape[-1] // count
    flip = odd("seq", 1)
    blocks = [value[..., at * width : (at + 1) * width] for at in range(count)]
    picked = [jnp.where(flip, blocks[at], blocks[at + 1]) for at in range(0, count, 2)]
    local = jnp.concatenate(picked, axis=-1).reshape(-1, value.shape[-1] // 2)
    return tp_gather(swapped(after(local, anchor), "seq", 1))


def store_products(out_ref, at, count, total):
    parts, block, width = out_ref.shape[0], out_ref.shape[1], out_ref.shape[2] // count
    for part in range(parts):
        rows = total[part * block : (part + 1) * block]
        out_ref[part, :, at * width : (at + 1) * width] = rows.astype(LOW)


def product(left, right):
    return lax.dot_general(left, right, (((0,), (0,)), ((), ())), preferred_element_type=F32)


def pair_kernel(count, side_ref, *refs):
    for at in range(count):
        left, left_other, right, right_other = (ref[...] for ref in refs[4 * at : 4 * at + 4])
        total = product(left, right) + product(left_other, right_other)
        store_products(refs[-1], at, count, total)


def plain_kernel(count, *refs):
    for at in range(count):
        total = product(refs[2 * at][...], refs[2 * at + 1][...])
        store_products(refs[-1], at, count, total)


def product_params(rows, width, total):
    return dict(
        compiler_params=pltpu.CompilerParams(
            dimension_semantics=("arbitrary",), vmem_limit_bytes=56 * 1024 * 1024
        ),
        cost_estimate=pl.CostEstimate(
            flops=2 * rows * width * total, bytes_accessed=4 * rows * total, transcendentals=0
        ),
    )


def own_half(value, other=0):
    count = lax.axis_size("seq")
    width = value.shape[-1] // count
    flip = odd("seq", 1)
    blocks = [value[..., at * width : (at + 1) * width] for at in range(count)]
    picked = [
        jnp.where(flip, blocks[at + 1 - other], blocks[at + other]) for at in range(0, count, 2)
    ]
    return jnp.concatenate(picked, axis=-1)


def pair_products(pieces):
    rows, width = pieces[0][0].shape
    channels = pieces[0][2].shape[1]
    parts = lax.axis_size("seq")
    block = width // parts
    group = max(1, LANES // block)
    side = (lax.axis_index("seq") % 2).astype(jnp.int32).reshape(1)
    specs, operands = [], []
    contiguous = pl.BlockSpec((rows, block * group), lambda at, side: (0, at))
    strided = pl.BlockSpec((rows, block), lambda at, side: (0, 2 * at + side[0]))
    full = pl.BlockSpec((rows, channels), lambda at, side: (0, 0))
    for left, left_other, right, right_other in pieces:
        specs += [strided if group == 1 else contiguous, contiguous, full, full]
        operands += [left if group == 1 else own_half(left), left_other, right, right_other]
    total = len(pieces) * channels
    return pl.pallas_call(
        functools.partial(pair_kernel, len(pieces)),
        grid_spec=pltpu.PrefetchScalarGridSpec(
            num_scalar_prefetch=1,
            grid=(parts // 2 // group,),
            in_specs=specs,
            out_specs=pl.BlockSpec((group, block, total), lambda at, side: (at, 0, 0)),
        ),
        out_shape=jax.ShapeDtypeStruct((parts // 2, block, total), LOW),
        **product_params(rows, width, total),
    )(side, *operands)


def plain_products(pieces):
    rows, width = pieces[0][0].shape
    channels = pieces[0][1].shape[1]
    parts = lax.axis_size("seq")
    block = width // parts
    group = max(1, LANES // block)
    total = len(pieces) * channels
    specs = [
        pl.BlockSpec((rows, block * group), lambda at: (0, at)),
        pl.BlockSpec((rows, channels), lambda at: (0, 0)),
    ] * len(pieces)
    return pl.pallas_call(
        functools.partial(plain_kernel, len(pieces)),
        grid=(parts // group,),
        in_specs=specs,
        out_specs=pl.BlockSpec((group, block, total), lambda at: (at, 0, 0)),
        out_shape=jax.ShapeDtypeStruct((parts, block, total), LOW),
        **product_params(rows, width, total),
    )(*[operand for piece in pieces for operand in piece])


def line_scatter(value):
    count = lax.axis_size("seq")
    groups = [list(range(side, count, 2)) for side in range(2)]
    return lax.psum_scatter(
        value, "seq", scatter_dimension=0, axis_index_groups=groups, tiled=True
    )[0]


def line_task(make):
    anchor = yield
    value = make(anchor)
    long = lax.axis_size("seq") // 2
    place = lax.axis_index("seq") // 2
    pairs = lambda sources, move: [
        (2 * source + side, 2 * (source + move) + side) for source in sources for side in range(2)
    ]
    pick = lambda at: lax.dynamic_index_in_dim(value, jnp.clip(at, 0, long - 1), 0, False)
    right, left = None, None
    for step in range(1, long):
        ahead = pick(place + long - step)
        behind = pick(place - long + step)
        if right is not None:
            right, left, anchor = lax.optimization_barrier((right, left, anchor))
            ahead = (ahead.astype(F32) + right.astype(F32)).astype(LOW)
            behind = (behind.astype(F32) + left.astype(F32)).astype(LOW)
        right = lax.ppermute(ahead, "seq", pairs(range(min(step, long - 1)), 1))
        left = lax.ppermute(behind, "seq", pairs(range(max(long - step, 1), long), -1))
        anchor = yield anchor
    own = pick(place).astype(F32)
    if right is not None:
        right, left, anchor = lax.optimization_barrier((right, left, anchor))
        own = own + right.astype(F32) + left.astype(F32)
    return own, anchor


def advance(tasks, results, anchor):
    if not tasks:
        return anchor
    name, task = tasks[0]
    try:
        return task.send(anchor)
    except StopIteration as ended:
        results[name], anchor = ended.value
        tasks.pop(0)
        return advance(tasks, results, anchor)


def add_task(tasks, name, make):
    task = line_task(make)
    next(task)
    tasks.append((name, task))


def small_task(scattered, summed):
    anchor = yield
    scattered, summed, anchor = lax.optimization_barrier((scattered, summed, anchor))
    bit = 1
    rows, channels = scattered.shape[1:]
    while bit < lax.axis_size("seq"):
        flip = odd("seq", bit)
        parted = scattered.reshape(-1, 2, rows, channels)
        low, high = parted[:, 0], parted[:, 1]
        sent = jnp.where(flip, low, high).astype(LOW).reshape(-1, channels)
        got = swapped(jnp.concatenate([sent, summed.astype(LOW)], axis=0), "seq", bit)
        anchor = yield anchor
        got, anchor = lax.optimization_barrier((got, anchor))
        scattered = jnp.where(flip, high, low).astype(F32)
        scattered = scattered + got[: sent.shape[0]].astype(F32).reshape(scattered.shape)
        summed = summed + got[sent.shape[0] :].astype(F32)
        bit *= 2
    return (scattered[0], summed), anchor


def gated_silu(argument):
    return argument * jax.nn.sigmoid(argument)


def silu_slope(argument):
    logistic = jax.nn.sigmoid(argument)
    return logistic * (1.0 + argument * (1.0 - logistic))


def doc_masks(doc_lengths, doc_offsets, positions):
    before = doc_offsets[:, None, :] <= positions[None, :, None]
    starts = jnp.max(jnp.where(before, doc_offsets[:, None, :], 0), axis=2)
    doc_ends = jnp.max(
        jnp.where(before, doc_offsets[:, None, :] + doc_lengths[:, None, :], 0), axis=2
    )
    return (starts, (positions[None, :] < doc_ends).astype(F32))


def matmul(left, right, dims):
    return jnp.einsum(dims, left, right, preferred_element_type=F32)


def conv_forward(conv_in, previous, conv_weight, conv_bias, tap_masks):
    edge = conv_weight.shape[0] - 1
    rows = conv_in.shape[1]
    extended = jnp.concatenate([previous, conv_in], axis=1).astype(F32)
    running = conv_bias.astype(F32)
    for back in range(edge + 1):
        window = extended[:, edge - back : edge - back + rows]
        running = running + conv_weight[back].astype(F32) * window * tap_masks[back][:, :, None]
    return (extended, running)


def rows_of(value):
    return value.reshape(-1, value.shape[-1])


def forward_layer(hidden, weights, valid_mask, keep_lanes, tap_masks, side, inverse_gain, limit):
    gain, input_w, conv_weight, conv_bias, select_w, step_w, step_bias, skip, out_w = weights
    width = input_w.shape[0]
    scaled = (hidden * gain.astype(F32)).astype(LOW)
    complete, input_w = tp_gather(scaled, input_w)
    unscaled = complete.astype(F32) * inverse_gain
    square_sums = jnp.sum(unscaled * unscaled, axis=2)
    inverse_norm = lax.rsqrt(square_sums / width + norm_epsilon)
    normed_other = None if side is None else other_half(scaled, complete)
    projected = matmul(complete, input_w, "bph,htg->bptg")
    projected = (projected * inverse_norm[:, :, None, None]).astype(LOW)
    conv_in, gate_in = projected[:, :, 0, :], projected[:, :, 1, :]
    edge = conv_weight.shape[0] - 1
    rows = hidden.shape[1]
    previous = shifted(conv_in[:, rows - edge :], "seq", 1)
    extended, conv_out = conv_forward(conv_in, previous, conv_weight, conv_bias, tap_masks)
    conv_act = gated_silu(conv_out).astype(LOW)
    selection = tp_sum(matmul(conv_act, select_w, "mri,ic->mrc"), LOW)
    rank = step_w.shape[0]
    states = (selection.shape[2] - rank) // 2
    low_rank = selection[:, :, :rank].astype(LOW)
    key_state = selection[:, :, rank : rank + states]
    biased = matmul(low_rank, step_w, "mrk,ki->mri") + step_bias
    step_size = jax.nn.softplus(biased)
    key_norm = jnp.sum(key_state * key_state, axis=2)
    rate = step_size / (1.0 + step_size * key_norm[:, :, None])
    side_rows = None if side is None else tp_gather(after(side, rate))
    summary = run_summary(rate, conv_act, selection, keep_lanes, states).astype(F32)
    decay_total, local_state = summary[:, :states], summary[:, states:]
    incoming = scan_exclusive(decay_total, local_state, 1)
    if side is not None:
        incoming, normed_other = lax.optimization_barrier((incoming, normed_other))
    skip_row = skip.astype(F32)[None]
    kept_states, mixed, gated = run_forward(
        rate, conv_act, selection, keep_lanes, gate_in, skip_row, incoming, states, limit
    )
    if side is not None:
        gated, side_rows = lax.optimization_barrier((gated, side_rows))
    finish = lambda rows: hidden + valid_mask[:, :, None] * tp_scatter(
        matmul(rows, out_w, "mri,id->mrd").astype(LOW)
    )
    kept = dict(
        hidden=hidden,
        inverse_norm=inverse_norm,
        complete=complete,
        normed_other=normed_other,
        conv_in=conv_in,
        gate_in=gate_in,
        extended=extended,
        conv_out=conv_out,
        conv_act=conv_act,
        low_rank=low_rank,
        selection=selection,
        biased=biased,
        key_norm=key_norm,
        rate=rate,
        decay_total=decay_total,
        incoming=incoming,
        kept_states=kept_states,
        mixed=mixed,
        gated=gated,
    )
    return (finish, kept, input_w, side_rows)


def backward_layer(
    at,
    grad_new,
    weights,
    kept,
    valid_mask,
    keep_lanes,
    tap_masks,
    tasks,
    results,
    waiting,
    ready,
    gated_other,
):
    gain, input_w, conv_weight, conv_bias, select_w, step_w, step_bias, skip, out_w = weights
    hidden, inverse_norm, rate, selection = (
        kept[name] for name in ("hidden", "inverse_norm", "rate", "selection")
    )
    conv_act = kept["conv_act"]
    width = input_w.shape[0]
    rank = step_w.shape[0]
    states = (selection.shape[2] - rank) // 2
    skip_row = skip.astype(F32)[None]
    first = waiting is not None
    if ready is None:
        branch_local = (grad_new * valid_mask[:, :, None]).astype(LOW)
        branch_rows, last = tp_gather(branch_local, waiting[3][1])
        waiting = waiting[:3] + (jnp.concatenate([waiting[3][0], last], axis=0),)
    else:
        branch_rows = ready
    grad_gated = matmul(branch_rows, out_w, "mrd,id->mri")
    gate_in = kept["gate_in"].astype(F32)
    grad_mixed = grad_gated * gated_silu(gate_in)
    inverse = inverse_norm[:, :, None]
    grad_gate = grad_gated * kept["mixed"].astype(F32) * silu_slope(gate_in) * inverse
    grad_gate = grad_gate.astype(LOW)
    act_float = conv_act.astype(F32)
    skip_grad = jnp.sum(grad_mixed * act_float, axis=(0, 1))
    normed = rows_of(kept["complete"])
    local_carry = run_adjoint(rate, grad_mixed, selection, keep_lanes, states)
    if first:
        branch_other = swapped(own_half(rows_of(branch_rows), 1), "seq", 1)
        inside = {1: pair_products([waiting]), 4: branch_other}
        carried = scan_exclusive(kept["decay_total"], local_carry.astype(F32), -1, inside)
        carried, results[("early", at + 1)] = lax.optimization_barrier(
            (carried, results[("early", at + 1)])
        )
        results[("conv", at + 1)] = line_scatter(inside[1]).astype(F32)
    else:
        local_carry, gated_other = lax.optimization_barrier((local_carry, gated_other))
        carried = scan_exclusive(kept["decay_total"], local_carry.astype(F32), -1)
        partial = plain_products(
            [
                (normed, rows_of(grad_gate)),
                (rows_of(branch_rows), rows_of(kept["gated"])),
            ]
        )
        carried, partial = lax.optimization_barrier((carried, partial))
        results[("early", at)] = lax.psum_scatter(
            partial, "seq", scatter_dimension=0, tiled=True
        )[0]
    grad_rate, grad_act, sums = run_backward(
        rate,
        conv_act,
        grad_mixed,
        selection,
        keep_lanes,
        skip_row,
        kept["kept_states"],
        kept["incoming"],
        carried,
        states,
        2 * VMEM_BYTES,
    )
    if first:
        gate_other = swapped(after(rows_of(grad_gate), carried), "seq", 1)
        grad_rate, gate_other = lax.optimization_barrier((grad_rate, gate_other))
        partial = pair_products(
            [
                (normed, kept["normed_other"], rows_of(grad_gate), gate_other),
                (rows_of(branch_rows), inside.get(4, branch_other), rows_of(kept["gated"]), gated_other),
            ]
        )
    else:
        normed_other = swapped(own_half(normed, 1), "seq", 1)
        grad_rate, normed_other = lax.optimization_barrier((grad_rate, normed_other))
    denominator = 1.0 + jax.nn.softplus(kept["biased"]) * kept["key_norm"][:, :, None]
    grad_step = grad_rate / (denominator * denominator)
    grad_norm_key = -jnp.sum(grad_rate * rate * rate, axis=2)
    grad_pre = grad_step * jax.nn.sigmoid(kept["biased"])
    stepbias_grad = jnp.sum(grad_pre, axis=(0, 1))
    grad_pre_low = grad_pre.astype(LOW)
    step_grad = matmul(kept["low_rank"], grad_pre_low, "mrk,mri->ki")
    padded = jnp.pad(step_w, ((0, 2 * states), (0, 0)))
    lanes = jnp.arange(selection.shape[2], dtype=jnp.int32)
    is_key = ((lanes >= rank) & (lanes < rank + states)).astype(F32)
    grad_selection = matmul(grad_pre_low, padded, "mri,ki->mrk") + sums
    grad_selection = grad_selection + 2.0 * is_key * selection * grad_norm_key[:, :, None]
    grad_selection = tp_sum(grad_selection, LOW)
    grad_selection = grad_selection.astype(LOW)
    if first:
        grad_selection, partial = lax.optimization_barrier((grad_selection, partial))
        results[("early", at)] = line_scatter(partial)
    select_full = matmul(grad_selection, conv_act, "mrc,mri->ci")
    grad_act = grad_act + matmul(grad_selection, select_w, "mrc,ic->mri")
    grad_conv = grad_act * silu_slope(kept["conv_out"])
    convbias_grad = jnp.sum(grad_conv, axis=(0, 1))
    edge = conv_weight.shape[0] - 1
    rows = grad_conv.shape[1]
    extended = kept["extended"]
    tap_grads = []
    grad_extended = jnp.zeros(extended.shape, F32)
    for back in range(edge + 1):
        masked = grad_conv * tap_masks[back][:, :, None]
        tap_grads.append(jnp.sum(masked * extended[:, edge - back : edge - back + rows], axis=(0, 1)))
        grad_extended = grad_extended + jnp.pad(
            masked * conv_weight[back].astype(F32), ((0, 0), (edge - back, back), (0, 0))
        )
    returned = shifted(grad_extended[:, :edge], "seq", -1)
    grad_conv_in = grad_extended[:, edge:] + jnp.pad(
        returned, ((0, 0), (rows - edge, 0), (0, 0))
    )
    grad_conv_in = (grad_conv_in * inverse).astype(LOW)
    conv_other = crossing(rows_of(grad_conv_in))
    if first:
        normed_other = kept["normed_other"]
    grad_projected = jnp.stack([grad_conv_in, grad_gate], axis=2)
    grad_normed = matmul(grad_projected, input_w, "bptg,htg->bph").astype(LOW)
    if first:
        grad_normed, conv_first = lax.optimization_barrier((grad_normed, conv_other[0]))
        grad_normed, conv_last = tp_scatter(grad_normed, conv_other[1])
        conv_other = jnp.concatenate([conv_first, conv_last], axis=0)
    else:
        grad_normed, conv_first = tp_scatter(grad_normed, conv_other[0])
        conv_other = (conv_first, conv_other[1])
    grad_normed = grad_normed.astype(F32)
    conv_piece = (normed, normed_other, rows_of(grad_conv_in), conv_other)
    inner = tp_sum(
        jnp.sum(
            grad_conv_in.astype(F32) * kept["conv_in"].astype(F32)
            + grad_gate.astype(F32) * gate_in,
            axis=2,
        ),
        F32,
    )
    gain_grad = jnp.sum(grad_normed * hidden, axis=(0, 1))
    grad_hidden = (
        grad_new
        + gain.astype(F32) * grad_normed
        - hidden * (inverse_norm * inner / width)[:, :, None]
    )
    count = lax.axis_size("seq")
    scattered = jnp.stack([select_full[:rank], step_grad], axis=0)
    scattered = scattered.reshape(2, count, rank // count, -1).swapaxes(0, 1)
    channels = conv_act.shape[2]
    summed = jnp.concatenate(
        [
            jnp.stack(tap_grads + [convbias_grad, stepbias_grad, skip_grad], axis=0),
            select_full[rank:],
            jnp.pad(gain_grad, (0, channels - gain_grad.shape[0]))[None],
        ],
        axis=0,
    )
    return (grad_hidden, conv_piece, gated_other, scattered, summed)


def on_device(
    tokens,
    norm_gain,
    input_weight,
    conv_weight,
    conv_bias,
    select_weight,
    step_weight,
    step_bias,
    skip_gain,
    out_weight,
    cotangent,
    doc_lengths,
    doc_offsets,
):
    rows = tokens.shape[1]
    positions = lax.axis_index("seq") * rows + jnp.arange(rows, dtype=jnp.int32)
    starts, valid_mask = doc_masks(doc_lengths, doc_offsets, positions)
    keep_mask = (positions[None, :] != starts).astype(F32)
    tap_masks = [
        (positions[None, :] - back >= starts).astype(F32) for back in range(conv_weight.shape[1])
    ]
    layers = input_weight.shape[0]
    keep_lanes = jnp.broadcast_to(keep_mask[:, :, None], keep_mask.shape + (LANES,))
    small = (conv_weight, conv_bias, select_weight, step_weight, step_bias, skip_gain, out_weight)
    shared = [tuple(member[at] for member in small) for at in range(layers)]
    hidden = tokens.astype(F32)
    grad = cotangent.astype(F32)
    side = (grad * valid_mask[:, :, None]).astype(LOW)
    inverse_gains = 1.0 / tp_gather(norm_gain.astype(F32))
    saved, inputs, ready = [], [None] * layers, None
    for at in range(layers):
        own = after(input_weight[at], hidden)
        finish, kept, inputs[at], extra = forward_layer(
            hidden,
            (norm_gain[at], own) + shared[at],
            valid_mask,
            keep_lanes,
            tap_masks,
            side if at == 0 else None,
            inverse_gains[at],
            2 * VMEM_BYTES,
        )
        ready = extra if at == 0 else ready
        saved.append(kept)
        if at + 1 < layers:
            hidden = finish(kept["gated"])
    tasks, results, waiting = [], {}, None
    passing = swapped(rows_of(saved[0]["gated"]), "seq", 1)
    scattered, summed = [None] * layers, [None] * layers
    for at in reversed(range(layers)):
        grad, waiting, passing, scattered[at], summed[at] = backward_layer(
            at,
            grad,
            (norm_gain[at], inputs[at]) + shared[at],
            saved[at],
            valid_mask,
            keep_lanes,
            tap_masks,
            tasks,
            results,
            waiting,
            ready if waiting is None else None,
            passing,
        )
    layer_out = finish(after(saved[-1]["gated"], grad)).astype(LOW)
    piece = waiting
    add_task(tasks, ("conv", 0), lambda anchor: pair_products([piece]))
    rank = step_weight.shape[1]
    count = lax.axis_size("seq")
    packed = jnp.stack(scattered, axis=1).reshape(count, -1, out_weight.shape[1])
    small = small_task(packed, jnp.concatenate(summed, axis=0))
    next(small)
    extra = [("small", small)]
    while tasks or extra:
        grad = advance(tasks, results, grad)
        grad = advance(extra, results, grad)
    scattered, summed = results["small"]
    scattered = scattered.reshape(layers, 2, rank // count, -1)
    summed = summed.reshape(layers, -1, summed.shape[1])
    channels = out_weight.shape[1]
    parts = [
        [results[("early", at)][:, piece * channels : (piece + 1) * channels] for piece in range(2)]
        for at in range(layers)
    ]
    conv_parts = [results[("conv", at)] for at in range(layers)]
    gate_parts = [parts[at][0].astype(F32) for at in range(layers)]
    out_parts = [parts[at][1].astype(F32) for at in range(layers)]
    edge = conv_weight.shape[1]
    blank = [jnp.zeros_like(conv_parts[0])] + conv_parts[1:]
    inweight_grad = jnp.stack(
        [jnp.stack([conv, gate], axis=1) for conv, gate in zip(blank, gate_parts)], axis=0
    )
    inweight_grad = lax.dynamic_update_slice(
        inweight_grad, conv_parts[0][None, :, None, :], (0, 0, 0, 0)
    )
    return (
        layer_out,
        grad.astype(LOW),
        summed[:, -1, : norm_gain.shape[1]],
        inweight_grad,
        summed[:, :edge],
        summed[:, edge],
        jnp.swapaxes(scattered[:, 0], 1, 2),
        jnp.swapaxes(summed[:, edge + 3 : -1], 1, 2),
        scattered[:, 1],
        summed[:, edge + 1],
        summed[:, edge + 2],
        jnp.swapaxes(jnp.stack(out_parts, axis=0), 1, 2),
    )


def solution(mesh):
    placed = (
        P(None, "seq", "tp"),
        P(None, "tp"),
        P(None, None, None, "tp"),
        P(None, None, "tp"),
        P(None, "tp"),
        P(None, "tp", None),
        P(None, None, "tp"),
        P(None, "tp"),
        P(None, "tp"),
        P(None, "tp", None),
        P(None, "seq", "tp"),
        P(),
        P(),
    )
    return jax.shard_map(
        on_device,
        mesh=mesh,
        in_specs=placed,
        out_specs=(
            P(None, "seq", "tp"),
            P(None, "seq", "tp"),
            P(None, "tp"),
            P(None, "seq", None, "tp"),
            P(None, None, "tp"),
            P(None, "tp"),
            P(None, "tp", "seq"),
            P(None, "tp", None),
            P(None, "seq", "tp"),
            P(None, "tp"),
            P(None, "tp"),
            P(None, "tp", "seq"),
        ),
        check_vma=False,
    )
```
